32 devices in a mesh: gy: 4 (over z), gx: 8 (over y, x, core).
Axes of the slice: x: 2, y: 2, z: 4, core: 2. Of those that a mesh axis runs over, the one named last changes fastest.
Arguments:
- field: bfloat16 [256, 128, 128], P('gy', 'gx'), may hold values from -8 to 8
- cotangent: bfloat16 [128, 64, 256], P('gy', 'gx'), may hold values from -6 to 6
- gain_fine: float32 [128], replicated, may hold values from 0.1 to 1.9
- weight_fine: bfloat16 [3, 3, 128, 128], replicated, may hold values from -0.1875 to 0.1875
- projection: bfloat16 [128, 256], replicated, may hold values from -0.5 to 0.5
- gain_coarse: float32 [256], replicated, may hold values from 0.1 to 1.9
- weight_coarse: bfloat16 [3, 3, 256, 256], replicated, may hold values from -0.125 to 0.125
Outputs:
- coarse_output: bfloat16 [128, 64, 256], P('gy', 'gx')
- field_grad: bfloat16 [256, 128, 128], P('gy', 'gx')
- fine_weight_grad: float32 [3, 3, 128, 128], replicated
- fine_gain_grad: float32 [128], replicated
- projection_grad: float32 [128, 256], replicated
- coarse_weight_grad: float32 [3, 3, 256, 256], replicated
- coarse_gain_grad: float32 [256], replicated
The draws below stay inside these ranges and needn't reach their ends.
All inputs are finite; a program needn't handle non-finite values.
Results may differ from the reference program's by a relative error of at most 0.014.
Values may be sent and summed in bfloat16 or wider, within the bound.
A program may use at most 64 MiB of HBM per device.

```python
import jax
import jax.numpy as jnp
from jax import lax

C1 = 128
C2 = 256
GROUPS = 32
ROWS = 256
COLS = 128


def draw_field(key, part):
    base_key = jax.random.fold_in(key, 11)
    noise_key, chan_key = jax.random.split(base_key, 2)
    noise = jax.random.normal(noise_key, (ROWS, COLS, C1), jnp.float32)
    row_pos = jnp.arange(ROWS, dtype=jnp.float32) / ROWS
    col_pos = jnp.arange(COLS, dtype=jnp.float32) / COLS
    ramp = jnp.exp(jnp.log(3.0) * 0.5 * (row_pos[:, None] + col_pos[None, :]))
    chan_scale = jnp.exp(jax.random.uniform(chan_key, (C1,), jnp.float32, -1.0, 1.0) * jnp.log(2.0))
    values = noise * ramp[:, :, None] * chan_scale[None, None, :] * 0.6
    return jnp.clip(values, -8.0, 8.0).astype(jnp.bfloat16)


def level_of(own_key, extent, cuts, smallest, high):
    level = 1.0
    for position, shards_of in cuts:
        draws = jax.random.uniform(jax.random.fold_in(jax.random.fold_in(own_key, 6), position), (shards_of,), jnp.float32, smallest / len(cuts), high / len(cuts))
        level = level * jnp.repeat(jnp.exp(draws), extent[position] // shards_of).reshape((-1,) + (1,) * (len(extent) - 1 - position))
    return level


def scatter_about(rng, shape, deviation, most, cuts=(), kind=jnp.bfloat16):
    values = jax.random.normal(rng, shape, jnp.float32) * deviation
    if len(cuts) > 0:
        values = level_of(rng, shape, cuts, -0.22, 0.18) * values
    return jnp.clip(values, min=-most, max=most).astype(kind)


def setup_inputs(seed: int = 0) -> dict:
    splits = jax.random.split(jax.random.key(seed), 8)
    return {
        "field": draw_field(jax.random.fold_in(splits[7], 71), 0),
        "cotangent": scatter_about(splits[1], (ROWS // 2, COLS // 2, C2), 1.0, 6.0, ((0, 4), (1, 8))),
        "gain_fine": jnp.clip(1.0 + 0.18 * jax.random.normal(splits[2], (C1,), jnp.float32), 0.1, 1.9),
        "weight_fine": scatter_about(splits[3], (3, 3, C1, C1), (9 * C1) ** -0.5, 0.1875),
        "projection": scatter_about(splits[4], (C1, C2), C1 ** -0.5, 0.5),
        "gain_coarse": jnp.clip(1.0 + 0.18 * jax.random.normal(splits[5], (C2,), jnp.float32), 0.1, 1.9),
        "weight_coarse": scatter_about(splits[6], (3, 3, C2, C2), (9 * C2) ** -0.5, 0.125),
    }


EPSILON = 1e-05

def conv_forward(padded, weight, height, width):
    channels = padded.shape[2]
    total = jnp.zeros((height * width, weight.shape[3]), jnp.float32)
    for row_tap in range(3):
        for col_tap in range(3):
            window = padded[row_tap:row_tap + height, col_tap:col_tap + width].reshape(height * width, channels)
            total = total + jnp.dot(window, weight[row_tap, col_tap], preferred_element_type=jnp.float32)
    return total.reshape(height, width, weight.shape[3])

def conv_transpose(padded, weight, height, width):
    channels = padded.shape[2]
    total = jnp.zeros((height * width, weight.shape[2]), jnp.float32)
    for row_tap in range(3):
        for col_tap in range(3):
            window = padded[2 - row_tap:2 - row_tap + height, 2 - col_tap:2 - col_tap + width].reshape(height * width, channels)
            total = total + jnp.dot(window, weight[row_tap, col_tap].T, preferred_element_type=jnp.float32)
    return total.reshape(height, width, weight.shape[2])

def conv_weight(padded, grads, height, width):
    channels = padded.shape[2]
    flat_grads = grads.reshape(height * width, grads.shape[2])
    taps = []
    for row_tap in range(3):
        for col_tap in range(3):
            window = padded[row_tap:row_tap + height, col_tap:col_tap + width].reshape(height * width, channels)
            taps.append(lax.dot_general(window, flat_grads, (((0,), (0,)), ((), ())), preferred_element_type=jnp.float32))
    return jnp.stack(taps).reshape(3, 3, channels, grads.shape[2])

def pad_zero(values):
    return jnp.pad(values, ((1, 1), (1, 1), (0, 0)))

def normalize(values):
    channels = values.shape[2]
    grouped = values.reshape(-1, GROUPS, channels // GROUPS)
    count = grouped.shape[0] * grouped.shape[2]
    average = lax.optimization_barrier(jnp.sum(grouped, axis=(0, 2))) / count
    variance = lax.optimization_barrier(jnp.sum(grouped * grouped, axis=(0, 2))) / count - average * average
    inverse = lax.rsqrt(variance + EPSILON)
    normed = (grouped - average[None, :, None]) * inverse[None, :, None]
    return (normed.reshape(values.shape), inverse)

def norm_backward(dnorm, normed, inverse):
    channels = normed.shape[2]
    dgroup = dnorm.reshape(-1, GROUPS, channels // GROUPS)
    ngroup = normed.reshape(-1, GROUPS, channels // GROUPS)
    count = dgroup.shape[0] * dgroup.shape[2]
    first = lax.optimization_barrier(jnp.sum(dgroup, axis=(0, 2))) / count
    second = lax.optimization_barrier(jnp.sum(dgroup * ngroup, axis=(0, 2))) / count
    result = inverse[None, :, None] * (dgroup - first[None, :, None] - ngroup * second[None, :, None])
    return result.reshape(normed.shape)

def silu_slope(act):
    sigma = jax.nn.sigmoid(act)
    return sigma * (1.0 + act * (1.0 - sigma))

def reference(field, cotangent, gain_fine, weight_fine, projection, gain_coarse, weight_coarse):
    height, width, chan_fine = field.shape
    chan_coarse = projection.shape[1]
    half_h, half_w = (height // 2, width // 2)
    values = field.astype(jnp.float32)
    normed_fine, inverse_fine = normalize(values)
    act_fine = normed_fine * gain_fine
    hidden_fine = jax.nn.silu(act_fine).astype(jnp.bfloat16)
    padded_fine = pad_zero(hidden_fine)
    block_fine = (values + conv_forward(padded_fine, weight_fine, height, width)).astype(jnp.bfloat16)
    pooled = lax.optimization_barrier(jnp.mean(block_fine.astype(jnp.float32).reshape(half_h, 2, half_w, 2, chan_fine), axis=(1, 3))).astype(jnp.bfloat16)
    coarse_in = jnp.dot(pooled.reshape(-1, chan_fine), projection, preferred_element_type=jnp.float32).reshape(half_h, half_w, chan_coarse).astype(jnp.bfloat16)
    coarse_vals = coarse_in.astype(jnp.float32)
    normed_coarse, inverse_coarse = normalize(coarse_vals)
    act_coarse = normed_coarse * gain_coarse
    hidden_coarse = jax.nn.silu(act_coarse).astype(jnp.bfloat16)
    padded_coarse = pad_zero(hidden_coarse)
    coarse_output = (coarse_vals + conv_forward(padded_coarse, weight_coarse, half_h, half_w)).astype(jnp.bfloat16)
    coarse_weight_grad = conv_weight(padded_coarse, cotangent, half_h, half_w)
    dact_coarse = conv_transpose(pad_zero(cotangent), weight_coarse, half_h, half_w) * silu_slope(act_coarse)
    coarse_gain_grad = lax.optimization_barrier(jnp.sum((dact_coarse * normed_coarse).reshape(-1, chan_coarse), axis=0))
    dcoarse = (cotangent.astype(jnp.float32) + norm_backward(dact_coarse * gain_coarse, normed_coarse, inverse_coarse)).astype(jnp.bfloat16)
    projection_grad = lax.dot_general(pooled.reshape(-1, chan_fine), dcoarse.reshape(-1, chan_coarse), (((0,), (0,)), ((), ())), preferred_element_type=jnp.float32)
    dpool = jnp.dot(dcoarse.reshape(-1, chan_coarse), projection.T, preferred_element_type=jnp.float32).reshape(half_h, half_w, chan_fine)
    dblock = (jnp.broadcast_to(dpool[:, None, :, None, :], (half_h, 2, half_w, 2, chan_fine)).reshape(height, width, chan_fine) * 0.25).astype(jnp.bfloat16)
    fine_weight_grad = conv_weight(padded_fine, dblock, height, width)
    dact_fine = conv_transpose(pad_zero(dblock), weight_fine, height, width) * silu_slope(act_fine)
    fine_gain_grad = lax.optimization_barrier(jnp.sum((dact_fine * normed_fine).reshape(-1, chan_fine), axis=0))
    field_grad = (dblock.astype(jnp.float32) + norm_backward(dact_fine * gain_fine, normed_fine, inverse_fine)).astype(jnp.bfloat16)
    return (coarse_output, field_grad, fine_weight_grad, fine_gain_grad, projection_grad, coarse_weight_grad, coarse_gain_grad)
```

```python
import functools

import jax
import jax.numpy as jnp
from jax import lax
from jax.experimental import pallas as pl
from jax.experimental.pallas import tpu as pltpu
from jax.sharding import PartitionSpec as P

GROUPS = 32
EPSILON = 1e-05
F32 = jnp.float32
BF16 = jnp.bfloat16
MESH = pl.DeviceIdType.MESH
DIRS = ((1, 0), (-1, 0), (0, 1), (0, -1), (1, 1), (1, -1), (-1, 1), (-1, -1))


def round_up(value, unit):
    return -(-value // unit) * unit


def log2(value):
    assert value & (value - 1) == 0
    return value.bit_length() - 1


def cell_of(shape, pitch):
    index = lax.broadcasted_iota(jnp.int32, shape, 0)
    return lax.shift_right_logical(index, log2(pitch)), index & (pitch - 1)


def within(value, low, high):
    return (value >= low) & (value < high)


def group_sums(sums, per_group):
    channels = sums.shape[1]
    bits = log2(per_group)
    one = lax.broadcasted_iota(jnp.int32, (channels, channels), 0)
    two = lax.broadcasted_iota(jnp.int32, (channels, channels), 1)
    same = lax.shift_right_logical(one, bits) == lax.shift_right_logical(two, bits)
    padded = jnp.concatenate([sums, jnp.zeros((8 - sums.shape[0], channels), F32)], axis=0)
    total = jnp.dot(
        padded, same.astype(F32), precision=lax.Precision.HIGHEST, preferred_element_type=F32
    )
    return total


def matmul_nt(left, right):
    return lax.dot_general(left, right, (((1,), (1,)), ((), ())), preferred_element_type=F32)


def matmul_tn(left, right):
    return lax.dot_general(left, right, (((0,), (0,)), ((), ())), preferred_element_type=F32)


def split_rows(sums):
    return jnp.concatenate([sums[:, :128], sums[:, 128:]], axis=0)


class Reducer:
    def __init__(self, levels, rows, data, full, landings, sends, recvs):
        self.levels, self.rows = levels, rows
        self.data, self.full, self.landings = data, full, landings
        self.sends, self.recvs = sends, recvs

    def span(self, base, count):
        return pl.ds(pl.multiple_of(base, 16), count)

    def offset(self, depth):
        base, size = 0, self.rows
        for _, count, index, _ in self.levels[:depth]:
            size //= count
            base = base + index * size
        return base, size

    def copies(self, stage):
        depth = len(self.levels)
        gather = stage >= depth
        level = 2 * depth - 1 - stage if gather else stage
        _, count, index, device = self.levels[level]
        base, size = self.offset(level)
        part = size // count
        out = []
        for step in range(1, count):
            peer = lax.rem(index + step, count)
            if gather:
                own = self.full.at[self.span(base + index * part, part)]
                src, dst, theirs = own, own, self.full.at[self.span(base + peer * part, part)]
            else:
                src = self.data.at[self.span(base + peer * part, part)]
                dst = self.landings[level].at[index]
                theirs = self.landings[level].at[peer]
            out.append((
                pltpu.make_async_remote_copy(
                    src_ref=src, dst_ref=dst,
                    send_sem=self.sends.at[stage, step], recv_sem=self.recvs.at[stage, index],
                    device_id=device(peer), device_id_type=MESH,
                ),
                pltpu.make_async_remote_copy(
                    src_ref=theirs, dst_ref=theirs,
                    send_sem=self.sends.at[stage, step], recv_sem=self.recvs.at[stage, peer],
                    device_id=device(peer), device_id_type=MESH,
                ),
            ))
        return out

    def start(self, stage):
        for copy, _ in self.copies(stage):
            copy.start()

    def finish(self, stage):
        depth = len(self.levels)
        for copy, arrival in self.copies(stage):
            copy.wait_send()
            arrival.wait_recv()
        if stage < depth:
            _, count, index, _ = self.levels[stage]
            base, size = self.offset(stage)
            part = size // count
            mine = self.span(base + index * part, part)
            landing = self.landings[stage]
            landing[index] = self.data[mine]
            total = landing[0].astype(F32)
            for source in range(1, count):
                total = total + landing[source].astype(F32)
            target = self.full if stage == depth - 1 else self.data
            target[mine] = total.astype(BF16)


def kernel(sizes, field, cot, gain_f, wf, proj, gain_c, wc,
           cout, fgrad, wf_grad, gf_grad, proj_grad, wc_grad, gc_grad,
           E, HF, X3f, PU, CI, HC, X3c, C, X3g, DC, D, X3d, T,
           row_out, col_out, row_in, col_in, slots,
           data_c, full_c, lc1, lc2, lc3, data_f, full_f, lf1, lf2, lf3,
           rim_send, rim_recv, sum_send, sum_recv, c_send, c_recv, f_send, f_recv):
    H, W, h, w, wp, wpc, ngy, ngx = sizes
    c1, c2 = proj.shape
    count_all = ngy * ngx
    gy, gx = lax.axis_index("gy"), lax.axis_index("gx")
    me = gy * ngx + gx
    fine_count = float(H * W * count_all * (c1 // GROUPS))
    coarse_count = float(h * w * count_all * (c2 // GROUPS))

    def peer_of(step):
        peer = lax.rem(me + step, count_all)
        return peer, (lax.div(peer, ngx), lax.rem(peer, ngx))

    barrier = pltpu.get_barrier_semaphore()

    @pl.loop(1, count_all)
    def _(step):
        pl.semaphore_signal(barrier, inc=1, device_id=peer_of(step)[1], device_id_type=MESH)

    def sum_copy(turn, step):
        peer, device = peer_of(step)
        go = pltpu.make_async_remote_copy(
            src_ref=slots.at[turn, me], dst_ref=slots.at[turn, me],
            send_sem=sum_send.at[step], recv_sem=sum_recv.at[turn % 2, me],
            device_id=device, device_id_type=MESH)
        come = pltpu.make_async_remote_copy(
            src_ref=slots.at[turn, peer], dst_ref=slots.at[turn, peer],
            send_sem=sum_send.at[step], recv_sem=sum_recv.at[turn % 2, peer],
            device_id=device, device_id_type=MESH)
        return go, come

    def sums_start(turn, rows):
        pad = jnp.zeros((8 - rows.shape[0], 128), F32)
        slots[turn, me] = jnp.concatenate([rows, pad], axis=0)

        @pl.loop(1, count_all)
        def _(step):
            sum_copy(turn, step)[0].start()

    def sums_finish(turn):
        @pl.loop(1, count_all)
        def _(step):
            go, come = sum_copy(turn, step)
            go.wait_send()
            come.wait_recv()
        return jnp.sum(slots[turn], axis=0)

    values = field[...].astype(F32)
    sums_f = jnp.concatenate([
        jnp.sum(values, axis=(0, 1), keepdims=True).reshape(1, c1),
        jnp.sum(values * values, axis=(0, 1), keepdims=True).reshape(1, c1)], axis=0)
    E[...] = jnp.zeros(E.shape, F32)
    E[pl.ds(3 * wp + 3, H * wp), :] = jnp.concatenate(
        [values, jnp.zeros((H, wp - W, c1), F32)], axis=1).reshape(H * wp, c1)
    grads = jnp.concatenate([cot[...].astype(F32), jnp.zeros((h, wpc - w, c2), F32)], axis=1)
    grads = grads.reshape(h * wpc, c2)
    C[...] = jnp.zeros(C.shape, F32)
    for half in range(2):
        C[half, pl.ds(2 * wpc + 2, h * wpc), :] = grads[:, half * 128:(half + 1) * 128]

    fr, cr = 3 * wp, 2 * wpc
    for side, (first, first_c) in enumerate(((H, h), (3, 2))):
        row_out[side, 0:fr] = E[first * wp:first * wp + fr].astype(BF16)
        for half in range(2):
            row_out[side, fr + half * cr:fr + (half + 1) * cr] = (
                C[half, first_c * wpc:first_c * wpc + cr].astype(BF16))
    for side, (first, first_c) in enumerate(((W, w), (3, 2))):
        for col in range(3):
            col_out[side, col * H:(col + 1) * H] = (
                E[pl.ds(3 * wp + first + col, H, stride=wp), :].astype(BF16))
        for half in range(2):
            for col in range(2):
                at = 3 * H + (2 * half + col) * h
                col_out[side, at:at + h] = (
                    C[half, pl.ds(2 * wpc + first_c + col, h, stride=wpc), :].astype(BF16))

    pl.semaphore_wait(barrier, count_all - 1)
    sums_start(0, sums_f)

    def rim_copy(number):
        dy, dx = DIRS[number]
        if dy != 0:
            src = row_out.at[0 if dy > 0 else 1]
            dst = row_in.at[number]
        else:
            src = col_out.at[0 if dx > 0 else 1]
            dst = col_in.at[number - 2]
        return pltpu.make_async_remote_copy(
            src_ref=src, dst_ref=dst, send_sem=rim_send.at[number], recv_sem=rim_recv.at[number],
            device_id=(gy + dy, gx + dx), device_id_type=MESH)

    def reaches(dy, dx):
        return within(gy + dy, 0, ngy) & within(gx + dx, 0, ngx)

    for number, (dy, dx) in enumerate(DIRS):
        @pl.when(reaches(dy, dx))
        def _():
            rim_copy(number).start()

    _, col_f = cell_of((fr, 128), wp)
    _, col_c = cell_of((cr, 128), wpc)

    def place(piece, dx, width, rim, cols):
        if dx == 0:
            return piece
        gap = jnp.zeros((width, 128), F32)
        if dx > 0:
            return jnp.where(cols < rim, jnp.concatenate([piece[width:], gap], axis=0), 0.0)
        moved = jnp.concatenate([gap, piece[:piece.shape[0] - width]], axis=0)
        return jnp.where(within(cols, width + rim, width + 2 * rim), moved, 0.0)

    for number, (dy, dx) in enumerate(DIRS):
        @pl.when(reaches(-dy, -dx))
        def _():
            rim_copy(number).wait_recv()
            if dy != 0:
                at = 0 if dy > 0 else (H + 3) * wp
                piece = row_in[number, 0:fr].astype(F32)
                E[at:at + fr] = E[at:at + fr] + place(piece, dx, W, 3, col_f)
                at = 0 if dy > 0 else (h + 2) * wpc
                for half in range(2):
                    piece = row_in[number, fr + half * cr:fr + (half + 1) * cr].astype(F32)
                    C[half, at:at + cr] = C[half, at:at + cr] + place(piece, dx, w, 2, col_c)
            else:
                at = 0 if dx > 0 else W + 3
                for col in range(3):
                    E[pl.ds(3 * wp + at + col, H, stride=wp), :] = (
                        col_in[number - 2, col * H:(col + 1) * H].astype(F32))
                at = 0 if dx > 0 else w + 2
                for half in range(2):
                    for col in range(2):
                        row = 3 * H + (2 * half + col) * h
                        C[half, pl.ds(2 * wpc + at + col, h, stride=wpc), :] = (
                            col_in[number - 2, row:row + h].astype(F32))

    ext = (h + 2) * wpc
    for tap in range(3):
        for half in range(2):
            at = tap * c2 + half * 128
            X3g[:, at:at + 128] = C[half, pl.ds(tap, (h + 4) * wpc), :].astype(BF16)
    raw = jnp.zeros((ext, c2), F32)
    for a in range(3):
        for b in range(3):
            raw = raw + matmul_nt(X3g[a * wpc:a * wpc + ext, b * c2:(b + 1) * c2],
                                  wc[2 - a, (2 - b) * c2:(3 - b) * c2, :])
    DC[...] = raw

    total = group_sums(sums_finish(0)[0:2], c1 // GROUPS)
    avg_f = total[0:1] / fine_count
    inv_f = lax.rsqrt(total[1:2] / fine_count - avg_f * avg_f + EPSILON)
    gain = gain_f[...]
    row, col = cell_of(E.shape, wp)
    inside = (within(row + (gy * H - 3), 0, H * ngy) & within(col + (gx * W - 3), 0, W * ngx))
    act = (E[...] - avg_f) * inv_f * gain
    HF[...] = jnp.where(inside, act / (1.0 + jnp.exp(-act)), 0.0)
    for tap in range(3):
        X3f[:, tap * c1:(tap + 1) * c1] = HF[pl.ds(tap, (H + 6) * wp), :].astype(BF16)
    span = (H + 4) * wp
    block = E[pl.ds(wp + 1, span), :]
    for a in range(3):
        block = block + jnp.dot(X3f[a * wp:a * wp + span, :], wf[a], preferred_element_type=F32)
    block = block.astype(BF16).astype(F32).reshape(h + 2, 2, wp, c1)
    PU[...] = (block[:, 0] + block[:, 1]).reshape((h + 2) * wp, c1)
    pooled = ((PU[pl.ds(0, ext, stride=2), :] + PU[pl.ds(1, ext, stride=2), :]) * 0.25)
    prow, pcol = cell_of((ext, c1), wpc)
    inner_p = within(prow, 1, h + 1) & within(pcol, 1, w + 1)
    pooled_in = jnp.where(inner_p, pooled, 0.0).astype(BF16)
    coarse_in = jnp.dot(pooled.astype(BF16), proj[...], preferred_element_type=F32)
    coarse_in = coarse_in.astype(BF16).astype(F32)
    CI[...] = coarse_in
    prow, pcol = cell_of((ext, c2), wpc)
    inner = within(prow, 1, h + 1) & within(pcol, 1, w + 1)
    kept = jnp.where(inner, coarse_in, 0.0)
    sums_start(1, split_rows(jnp.concatenate([
        jnp.sum(kept, axis=0, keepdims=True), jnp.sum(kept * kept, axis=0, keepdims=True)], axis=0)))

    def joined(rows):
        return jnp.concatenate([rows[0:2], rows[2:4]], axis=1)

    total = group_sums(joined(sums_finish(1)), c2 // GROUPS)
    avg_c = total[0:1] / coarse_count
    inv_c = lax.rsqrt(total[1:2] / coarse_count - avg_c * avg_c + EPSILON)
    gain2 = gain_c[...]
    inside_c = (within(prow + (gy * h - 1), 0, h * ngy) & within(pcol + (gx * w - 1), 0, w * ngx))
    norm_c = (CI[...] - avg_c) * inv_c
    act = norm_c * gain2
    sigma = 1.0 / (1.0 + jnp.exp(-act))
    dact_c = DC[...] * (sigma * (1.0 + act * (1.0 - sigma)))
    DC[...] = dact_c
    kept = jnp.where(inner, dact_c, 0.0)
    sums_start(2, split_rows(jnp.concatenate([
        jnp.sum(kept, axis=0, keepdims=True),
        jnp.sum(kept * norm_c, axis=0, keepdims=True)], axis=0)))

    HC[0:ext] = jnp.where(inside_c, act * sigma, 0.0)
    HC[ext:] = jnp.zeros((HC.shape[0] - ext, c2), F32)
    for tap in range(3):
        X3c[:, tap * c2:(tap + 1) * c2] = HC[pl.ds(tap, ext), :].astype(BF16)
    cells_c = h * wpc
    gb = grads.astype(BF16)
    taps_c = 3 * c2
    for a in range(3):
        part = matmul_tn(X3c[a * wpc:a * wpc + cells_c, :], gb).astype(BF16)
        for half in range(2):
            at = (3 * half + a) * taps_c
            data_c[at:at + taps_c] = part[:, half * 128:(half + 1) * 128]
    if data_c.shape[0] > 6 * taps_c:
        data_c[6 * taps_c:] = jnp.zeros((data_c.shape[0] - 6 * taps_c, 128), BF16)

    core, chip = lax.rem(gx, 2), lax.div(gx, 2)
    levels = (
        ("core", 2, core, lambda k: (gy, chip * 2 + k)),
        ("chip", ngx // 2, chip, lambda k: (gy, k * 2 + core)),
        ("gy", ngy, gy, lambda k: (k, gx)),
    )
    big = Reducer(levels, data_c.shape[0], data_c, full_c, (lc1, lc2, lc3), c_send, c_recv)
    small = Reducer(levels, data_f.shape[0], data_f, full_f, (lf1, lf2, lf3), f_send, f_recv)
    big.start(0)

    out = CI[pl.ds(wpc + 1, cells_c), :]
    for a in range(3):
        out = out + jnp.dot(X3c[a * wpc:a * wpc + cells_c, :], wc[a], preferred_element_type=F32)
    cout[...] = out.reshape(h, wpc, c2)[:, :w].astype(BF16)

    big.finish(0)
    big.start(1)

    total = joined(sums_finish(2))
    gc_grad[...] = total[1:2]
    total = group_sums(total[0:2] * gain2, c2 // GROUPS)
    first, second = total[0:1] / coarse_count, total[1:2] / coarse_count
    norm_c = (CI[...] - avg_c) * inv_c
    dcoarse = inv_c * (DC[...] * gain2 - first - norm_c * second)
    dcoarse = dcoarse + jnp.concatenate(
        [C[0, pl.ds(wpc + 1, ext), :], C[1, pl.ds(wpc + 1, ext), :]], axis=1)
    dcoarse = jnp.where(inside_c, dcoarse, 0.0).astype(BF16)
    pgrad = matmul_tn(pooled_in, dcoarse).astype(BF16)
    taps_f = 9 * c1
    for half in range(2):
        at = taps_f + half * c1
        data_f[at:at + c1] = pgrad[:, half * 128:(half + 1) * 128]
    if data_f.shape[0] > taps_f + 2 * c1:
        data_f[taps_f + 2 * c1:] = jnp.zeros((data_f.shape[0] - taps_f - 2 * c1, 128), BF16)
    dsmall = (matmul_nt(dcoarse, proj[...]) * 0.25).astype(BF16).astype(F32)
    PU[pl.ds(0, ext, stride=2), :] = dsmall
    PU[pl.ds(1, ext, stride=2), :] = dsmall
    wide = PU[...].reshape(h + 2, 1, wp, c1)
    D[0:span] = jnp.broadcast_to(wide, (h + 2, 2, wp, c1)).reshape(span, c1)
    D[span:] = jnp.zeros((D.shape[0] - span, c1), F32)
    for tap in range(3):
        X3d[:, tap * c1:(tap + 1) * c1] = D[pl.ds(tap, span), :].astype(BF16)
    cells_f = H * wp
    dact = jnp.zeros((cells_f, c1), F32)
    for a in range(3):
        for b in range(3):
            dact = dact + matmul_nt(X3d[(1 + a) * wp:(1 + a) * wp + cells_f, b * c1:(b + 1) * c1],
                                    wf[2 - a, (2 - b) * c1:(3 - b) * c1, :])
    norm_f = (E[pl.ds(3 * wp + 2, cells_f), :] - avg_f) * inv_f
    act = norm_f * gain
    sigma = 1.0 / (1.0 + jnp.exp(-act))
    dact = dact * (sigma * (1.0 + act * (1.0 - sigma)))
    _, col = cell_of((cells_f, c1), wp)
    kept = jnp.where(within(col, 1, W + 1), dact, 0.0)
    sums_start(3, jnp.concatenate([
        jnp.sum(kept, axis=0, keepdims=True),
        jnp.sum(kept * norm_f, axis=0, keepdims=True)], axis=0))
    T[0:cells_f] = dact

    big.finish(1)
    big.start(2)

    gm = jnp.where(within(col, 2, W + 2), D[2 * wp:2 * wp + cells_f], 0.0).astype(BF16)
    for a in range(3):
        part = matmul_tn(X3f[(2 + a) * wp:(2 + a) * wp + cells_f, :], gm)
        data_f[a * 3 * c1:(a + 1) * 3 * c1] = part.astype(BF16)
    small.start(0)
    big.finish(2)
    big.start(3)
    small.finish(0)
    small.start(1)

    total = sums_finish(3)[0:2]
    gf_grad[...] = total[1:2]
    total = group_sums(total * gain, c1 // GROUPS)
    first, second = total[0:1] / fine_count, total[1:2] / fine_count
    norm_f = (E[pl.ds(3 * wp + 2, cells_f), :] - avg_f) * inv_f
    result = inv_f * (T[0:cells_f] * gain - first - norm_f * second)
    T[0:cells_f] = result + D[pl.ds(2 * wp + 1, cells_f), :]
    T[cells_f:] = jnp.zeros((T.shape[0] - cells_f, c1), F32)
    fgrad[...] = T[pl.ds(1, cells_f), :].reshape(H, wp, c1)[:, :W].astype(BF16)

    big.finish(3)
    big.start(4)
    small.finish(1)
    small.start(2)
    small.finish(2)
    small.start(3)
    big.finish(4)
    big.start(5)
    small.finish(3)
    small.start(4)
    small.finish(4)
    small.start(5)
    big.finish(5)
    for half in range(2):
        at = 3 * half * taps_c
        wc_grad[:, half * 128:(half + 1) * 128] = full_c[at:at + 3 * taps_c].astype(F32)
    small.finish(5)
    wf_grad[...] = full_f[0:taps_f].astype(F32)
    for half in range(2):
        at = taps_f + half * c1
        proj_grad[:, half * 128:(half + 1) * 128] = full_f[at:at + c1].astype(F32)

    for number, (dy, dx) in enumerate(DIRS):
        @pl.when(reaches(dy, dx))
        def _():
            rim_copy(number).wait_send()


def on_device(field, cotangent, gain_fine, weight_fine, projection, gain_coarse, weight_coarse):
    H, W, c1 = field.shape
    h, w, c2 = cotangent.shape
    ngy, ngx = lax.axis_size("gy"), lax.axis_size("gx")
    everyone = ngy * ngx
    wpc = round_up(w + 4, 16)
    wp = 2 * wpc
    sizes = (H, W, h, w, wp, wpc, ngy, ngx)
    rows_c = everyone * round_up(-(-18 * c2 // everyone), 16)
    rows_f = everyone * round_up(-(-11 * c1 // everyone), 16)
    counts = (2, ngx // 2, ngy)
    most = max(counts)

    def landings(rows):
        out = []
        for count in counts:
            rows //= count
            out.append(pltpu.VMEM((count, rows, 128), BF16))
        return out

    DMA = pltpu.SemaphoreType.DMA
    scratch = [
        pltpu.VMEM(((H + 8) * wp, c1), F32),
        pltpu.VMEM(((H + 8) * wp, c1), F32),
        pltpu.VMEM(((H + 6) * wp, 3 * c1), BF16),
        pltpu.VMEM(((h + 2) * wp, c1), F32),
        pltpu.VMEM(((h + 2) * wpc, c2), F32),
        pltpu.VMEM(((h + 4) * wpc, c2), F32),
        pltpu.VMEM(((h + 2) * wpc, 3 * c2), BF16),
        pltpu.VMEM((2, (h + 6) * wpc, 128), F32),
        pltpu.VMEM(((h + 4) * wpc, 3 * c2), BF16),
        pltpu.VMEM(((h + 2) * wpc, c2), F32),
        pltpu.VMEM(((H + 6) * wp, c1), F32),
        pltpu.VMEM(((H + 4) * wp, 3 * c1), BF16),
        pltpu.VMEM(((H + 1) * wp, c1), F32),
        pltpu.VMEM((2, 3 * wp + 4 * wpc, 128), BF16),
        pltpu.VMEM((2, 3 * H + 4 * h, 128), BF16),
        pltpu.VMEM((8, 3 * wp + 4 * wpc, 128), BF16),
        pltpu.VMEM((2, 3 * H + 4 * h, 128), BF16),
        pltpu.VMEM((4, everyone, 8, 128), F32),
        pltpu.VMEM((rows_c, 128), BF16), pltpu.VMEM((rows_c, 128), BF16), *landings(rows_c),
        pltpu.VMEM((rows_f, 128), BF16), pltpu.VMEM((rows_f, 128), BF16), *landings(rows_f),
        DMA((8,)), DMA((8,)),
        DMA((everyone,)), DMA((2, everyone)),
        DMA((6, most)), DMA((6, most)),
        DMA((6, most)), DMA((6, most)),
    ]
    vmem = pl.BlockSpec(memory_space=pltpu.VMEM)
    shapes = (
        jax.ShapeDtypeStruct((h, w, c2), BF16),
        jax.ShapeDtypeStruct((H, W, c1), BF16),
        jax.ShapeDtypeStruct((9 * c1, c1), F32),
        jax.ShapeDtypeStruct((1, c1), F32),
        jax.ShapeDtypeStruct((c1, c2), F32),
        jax.ShapeDtypeStruct((9 * c2, c2), F32),
        jax.ShapeDtypeStruct((1, c2), F32),
    )
    cout, fgrad, wf_grad, gf_grad, proj_grad, wc_grad, gc_grad = pl.pallas_call(
        functools.partial(kernel, sizes),
        out_shape=shapes,
        in_specs=[vmem] * 7,
        out_specs=[vmem] * 7,
        scratch_shapes=scratch,
        compiler_params=pltpu.CompilerParams(
            collective_id=0, has_side_effects=True, vmem_limit_bytes=52 * 2**20),
    )(
        field, cotangent, gain_fine.reshape(1, c1), weight_fine.reshape(3, 3 * c1, c1),
        projection, gain_coarse.reshape(1, c2), weight_coarse.reshape(3, 3 * c2, c2),
    )
    return (
        cout, fgrad, wf_grad.reshape(3, 3, c1, c1), gf_grad.reshape(c1), proj_grad,
        wc_grad.reshape(3, 3, c2, c2), gc_grad.reshape(c2),
    )


def solution(mesh):
    return jax.shard_map(
        on_device,
        mesh=mesh,
        in_specs=(P("gy", "gx", None), P("gy", "gx", None), P(), P(), P(), P(), P()),
        out_specs=(P("gy", "gx", None), P("gy", "gx", None), P(), P(), P(), P(), P()),
        check_vma=False,
    )
```

```python
import functools

import jax
import jax.numpy as jnp
from jax import lax
from jax.experimental import pallas as pl
from jax.experimental.pallas import tpu as pltpu
from jax.sharding import PartitionSpec as P

GROUPS = 32
EPSILON = 1e-05
F32 = jnp.float32
BF16 = jnp.bfloat16
MESH = pl.DeviceIdType.MESH
DIRS = ((1, 0), (-1, 0), (0, 1), (0, -1), (1, 1), (1, -1), (-1, 1), (-1, -1))


def round_up(value, unit):
    return -(-value // unit) * unit


def log2(value):
    assert value & (value - 1) == 0
    return value.bit_length() - 1


def cell_of(shape, pitch):
    index = lax.broadcasted_iota(jnp.int32, shape, 0)
    return lax.shift_right_logical(index, log2(pitch)), index & (pitch - 1)


def within(value, low, high):
    return (value >= low) & (value < high)


def group_sums(sums, per_group):
    channels = sums.shape[1]
    bits = log2(per_group)
    one = lax.broadcasted_iota(jnp.int32, (channels, channels), 0)
    two = lax.broadcasted_iota(jnp.int32, (channels, channels), 1)
    same = lax.shift_right_logical(one, bits) == lax.shift_right_logical(two, bits)
    padded = jnp.concatenate([sums, jnp.zeros((8 - sums.shape[0], channels), F32)], axis=0)
    total = jnp.dot(
        padded, same.astype(F32), precision=lax.Precision.HIGHEST, preferred_element_type=F32
    )
    return total


def matmul_nt(left, right):
    return lax.dot_general(left, right, (((1,), (1,)), ((), ())), preferred_element_type=F32)


def matmul_tn(left, right):
    return lax.dot_general(left, right, (((0,), (0,)), ((), ())), preferred_element_type=F32)


def split_rows(sums):
    return jnp.concatenate([sums[:, :128], sums[:, 128:]], axis=0)


class Reducer:
    def __init__(self, levels, rows, data, full, landings, sends, recvs):
        self.levels, self.rows = levels, rows
        self.data, self.full, self.landings = data, full, landings
        self.sends, self.recvs = sends, recvs

    def span(self, base, count):
        return pl.ds(pl.multiple_of(base, 16), count)

    def offset(self, depth):
        base, size = 0, self.rows
        for _, count, index, _ in self.levels[:depth]:
            size //= count
            base = base + index * size
        return base, size

    def copies(self, stage):
        depth = len(self.levels)
        gather = stage >= depth
        level = 2 * depth - 1 - stage if gather else stage
        _, count, index, device = self.levels[level]
        base, size = self.offset(level)
        part = size // count
        out = []
        for step in range(1, count):
            peer = lax.rem(index + step, count)
            if gather:
                own = self.full.at[self.span(base + index * part, part)]
                src, dst, theirs = own, own, self.full.at[self.span(base + peer * part, part)]
            else:
                src = self.data.at[self.span(base + peer * part, part)]
                dst = self.landings[level].at[index]
                theirs = self.landings[level].at[peer]
            out.append((
                pltpu.make_async_remote_copy(
                    src_ref=src, dst_ref=dst,
                    send_sem=self.sends.at[stage, step], recv_sem=self.recvs.at[stage, index],
                    device_id=device(peer), device_id_type=MESH,
                ),
                pltpu.make_async_remote_copy(
                    src_ref=theirs, dst_ref=theirs,
                    send_sem=self.sends.at[stage, step], recv_sem=self.recvs.at[stage, peer],
                    device_id=device(peer), device_id_type=MESH,
                ),
            ))
        return out

    def start(self, stage):
        for copy, _ in self.copies(stage):
            copy.start()

    def finish(self, stage):
        depth = len(self.levels)
        for copy, arrival in self.copies(stage):
            copy.wait_send()
            arrival.wait_recv()
        if stage < depth:
            _, count, index, _ = self.levels[stage]
            base, size = self.offset(stage)
            part = size // count
            mine = self.span(base + index * part, part)
            landing = self.landings[stage]
            landing[index] = self.data[mine]
            total = landing[0].astype(F32)
            for source in range(1, count):
                total = total + landing[source].astype(F32)
            target = self.full if stage == depth - 1 else self.data
            target[mine] = total.astype(BF16)


def kernel(sizes, field_h, cot_h, gain_f_h, wf_h, proj_h, gain_c_h, wc_h,
           cout_h, fgrad_h, wf_grad_h, gf_grad_h, proj_grad_h, wc_grad_h, gc_grad_h,
           cout, fgrad, wf_grad, gf_grad, proj_grad, wc_grad, gc_grad, store_sem,
           field, cot, gain_f, wf, proj, gain_c, wc, load_sem,
           E, HF, X3f, PU, CI, HC, X3c, C, X3g, DC, D, X3d, T,
           row_out, col_out, row_in, col_in, slots,
           data_c, full_c, lc1, lc2, lc3, data_f, full_f, lf1, lf2, lf3,
           rim_send, rim_recv, sum_send, sum_recv, c_send, c_recv, f_send, f_recv):
    H, W, h, w, wp, wpc, ngy, ngx = sizes
    c1, c2 = proj.shape
    count_all = ngy * ngx
    gy, gx = lax.axis_index("gy"), lax.axis_index("gx")
    me = gy * ngx + gx
    fine_count = float(H * W * count_all * (c1 // GROUPS))
    coarse_count = float(h * w * count_all * (c2 // GROUPS))

    def wrapped(place, count):
        return jnp.where(place >= count, place - count, place)

    few = count_all <= 64
    if few:
        rows_of = [wrapped(gy + dy, ngy) for dy in range(ngy)]
        cols_of = [wrapped(gx + dx, ngx) for dx in range(ngx)]

    def peer_of(step):
        if few:
            place = (rows_of[step // ngx], cols_of[step % ngx])
            return place[0] * ngx + place[1], place
        peer = lax.rem(me + step, count_all)
        return peer, (lax.div(peer, ngx), lax.rem(peer, ngx))

    def each_peer(body):
        if few:
            for step in range(1, count_all):
                body(step)
        else:
            pl.loop(1, count_all)(body)

    loads = [
        pltpu.make_async_copy(src, dst, load_sem.at[number])
        for number, (src, dst) in enumerate(zip(
            (field_h, cot_h, gain_f_h, wf_h, proj_h, gain_c_h, wc_h),
            (field, cot, gain_f, wf, proj, gain_c, wc)))
    ]
    for number in (0, 1, 6, 2, 3, 4, 5):
        loads[number].start()
    stores = [
        pltpu.make_async_copy(src, dst, store_sem.at[number])
        for number, (src, dst) in enumerate(zip(
            (cout, fgrad, wf_grad, gf_grad, proj_grad, wc_grad, gc_grad),
            (cout_h, fgrad_h, wf_grad_h, gf_grad_h, proj_grad_h, wc_grad_h, gc_grad_h)))
    ]
    barrier = pltpu.get_barrier_semaphore()

    def greet(step):
        pl.semaphore_signal(barrier, inc=1, device_id=peer_of(step)[1], device_id_type=MESH)

    each_peer(greet)

    def sum_copy(turn, step):
        peer, device = peer_of(step)
        go = pltpu.make_async_remote_copy(
            src_ref=slots.at[turn, me], dst_ref=slots.at[turn, me],
            send_sem=sum_send.at[step], recv_sem=sum_recv.at[turn % 2, me],
            device_id=device, device_id_type=MESH)
        come = pltpu.make_async_remote_copy(
            src_ref=slots.at[turn, peer], dst_ref=slots.at[turn, peer],
            send_sem=sum_send.at[step], recv_sem=sum_recv.at[turn % 2, peer],
            device_id=device, device_id_type=MESH)
        return go, come

    def sums_start(turn, rows):
        pad = jnp.zeros((8 - rows.shape[0], 128), F32)
        slots[turn, me] = jnp.concatenate([rows, pad], axis=0)

        each_peer(lambda step: sum_copy(turn, step)[0].start())

    def sums_finish(turn):
        def settle(step):
            go, come = sum_copy(turn, step)
            go.wait_send()
            come.wait_recv()

        each_peer(settle)
        return jnp.sum(slots[turn], axis=0)

    loads[0].wait()
    values = field[...].astype(F32)
    sums_f = jnp.concatenate([
        jnp.sum(values, axis=(0, 1), keepdims=True).reshape(1, c1),
        jnp.sum(values * values, axis=(0, 1), keepdims=True).reshape(1, c1)], axis=0)
    E[...] = jnp.zeros(E.shape, F32)
    E[pl.ds(3 * wp + 3, H * wp), :] = jnp.concatenate(
        [values, jnp.zeros((H, wp - W, c1), F32)], axis=1).reshape(H * wp, c1)
    loads[1].wait()
    grads = jnp.concatenate([cot[...].astype(F32), jnp.zeros((h, wpc - w, c2), F32)], axis=1)
    grads = grads.reshape(h * wpc, c2)
    C[...] = jnp.zeros(C.shape, F32)
    for half in range(2):
        C[half, pl.ds(2 * wpc + 2, h * wpc), :] = grads[:, half * 128:(half + 1) * 128]

    fr, cr = 3 * wp, 2 * wpc
    for side, (first, first_c) in enumerate(((H, h), (3, 2))):
        row_out[side, 0:fr] = E[first * wp:first * wp + fr].astype(BF16)
        for half in range(2):
            row_out[side, fr + half * cr:fr + (half + 1) * cr] = (
                C[half, first_c * wpc:first_c * wpc + cr].astype(BF16))
    for side, (first, first_c) in enumerate(((W, w), (3, 2))):
        for col in range(3):
            col_out[side, col * H:(col + 1) * H] = (
                E[pl.ds(3 * wp + first + col, H, stride=wp), :].astype(BF16))
        for half in range(2):
            for col in range(2):
                at = 3 * H + (2 * half + col) * h
                col_out[side, at:at + h] = (
                    C[half, pl.ds(2 * wpc + first_c + col, h, stride=wpc), :].astype(BF16))

    pl.semaphore_wait(barrier, count_all - 1)
    sums_start(0, sums_f)

    def rim_copy(number):
        dy, dx = DIRS[number]
        if dy != 0:
            src = row_out.at[0 if dy > 0 else 1]
            dst = row_in.at[number]
        else:
            src = col_out.at[0 if dx > 0 else 1]
            dst = col_in.at[number - 2]
        return pltpu.make_async_remote_copy(
            src_ref=src, dst_ref=dst, send_sem=rim_send.at[number], recv_sem=rim_recv.at[number],
            device_id=(gy + dy, gx + dx), device_id_type=MESH)

    def reaches(dy, dx):
        return within(gy + dy, 0, ngy) & within(gx + dx, 0, ngx)

    for number, (dy, dx) in enumerate(DIRS):
        @pl.when(reaches(dy, dx))
        def _():
            rim_copy(number).start()

    _, col_f = cell_of((fr, 128), wp)
    _, col_c = cell_of((cr, 128), wpc)

    def place(piece, dx, width, rim, cols):
        if dx == 0:
            return piece
        gap = jnp.zeros((width, 128), F32)
        if dx > 0:
            return jnp.where(cols < rim, jnp.concatenate([piece[width:], gap], axis=0), 0.0)
        moved = jnp.concatenate([gap, piece[:piece.shape[0] - width]], axis=0)
        return jnp.where(within(cols, width + rim, width + 2 * rim), moved, 0.0)

    for number, (dy, dx) in enumerate(DIRS):
        @pl.when(reaches(-dy, -dx))
        def _():
            rim_copy(number).wait_recv()
            if dy != 0:
                at = 0 if dy > 0 else (H + 3) * wp
                piece = row_in[number, 0:fr].astype(F32)
                E[at:at + fr] = E[at:at + fr] + place(piece, dx, W, 3, col_f)
                at = 0 if dy > 0 else (h + 2) * wpc
                for half in range(2):
                    piece = row_in[number, fr + half * cr:fr + (half + 1) * cr].astype(F32)
                    C[half, at:at + cr] = C[half, at:at + cr] + place(piece, dx, w, 2, col_c)
            else:
                at = 0 if dx > 0 else W + 3
                for col in range(3):
                    E[pl.ds(3 * wp + at + col, H, stride=wp), :] = (
                        col_in[number - 2, col * H:(col + 1) * H].astype(F32))
                at = 0 if dx > 0 else w + 2
                for half in range(2):
                    for col in range(2):
                        row = 3 * H + (2 * half + col) * h
                        C[half, pl.ds(2 * wpc + at + col, h, stride=wpc), :] = (
                            col_in[number - 2, row:row + h].astype(F32))

    ext = (h + 2) * wpc
    for tap in range(3):
        for half in range(2):
            at = tap * c2 + half * 128
            X3g[:, at:at + 128] = C[half, pl.ds(tap, (h + 4) * wpc), :].astype(BF16)
    loads[6].wait()
    raw = jnp.zeros((ext, c2), F32)
    for a in range(3):
        for b in range(3):
            raw = raw + matmul_nt(X3g[a * wpc:a * wpc + ext, b * c2:(b + 1) * c2],
                                  wc[2 - a, (2 - b) * c2:(3 - b) * c2, :])
    DC[...] = raw

    for number in (2, 3, 4, 5):
        loads[number].wait()
    total = group_sums(sums_finish(0)[0:2], c1 // GROUPS)
    avg_f = total[0:1] / fine_count
    inv_f = lax.rsqrt(total[1:2] / fine_count - avg_f * avg_f + EPSILON)
    gain = gain_f[...]
    row, col = cell_of(E.shape, wp)
    inside = (within(row + (gy * H - 3), 0, H * ngy) & within(col + (gx * W - 3), 0, W * ngx))
    act = (E[...] - avg_f) * inv_f * gain
    HF[...] = jnp.where(inside, act / (1.0 + jnp.exp(-act)), 0.0)
    for tap in range(3):
        X3f[:, tap * c1:(tap + 1) * c1] = HF[pl.ds(tap, (H + 6) * wp), :].astype(BF16)
    span = (H + 4) * wp
    block = E[pl.ds(wp + 1, span), :]
    for a in range(3):
        block = block + jnp.dot(X3f[a * wp:a * wp + span, :], wf[a], preferred_element_type=F32)
    block = block.astype(BF16).astype(F32).reshape(h + 2, 2, wp, c1)
    PU[...] = (block[:, 0] + block[:, 1]).reshape((h + 2) * wp, c1)
    pooled = ((PU[pl.ds(0, ext, stride=2), :] + PU[pl.ds(1, ext, stride=2), :]) * 0.25)
    prow, pcol = cell_of((ext, c1), wpc)
    inner_p = within(prow, 1, h + 1) & within(pcol, 1, w + 1)
    pooled_in = jnp.where(inner_p, pooled, 0.0).astype(BF16)
    coarse_in = jnp.dot(pooled.astype(BF16), proj[...], preferred_element_type=F32)
    coarse_in = coarse_in.astype(BF16).astype(F32)
    CI[...] = coarse_in
    prow, pcol = cell_of((ext, c2), wpc)
    inner = within(prow, 1, h + 1) & within(pcol, 1, w + 1)
    kept = jnp.where(inner, coarse_in, 0.0)
    sums_start(1, split_rows(jnp.concatenate([
        jnp.sum(kept, axis=0, keepdims=True), jnp.sum(kept * kept, axis=0, keepdims=True)], axis=0)))

    def joined(rows):
        return jnp.concatenate([rows[0:2], rows[2:4]], axis=1)

    total = group_sums(joined(sums_finish(1)), c2 // GROUPS)
    avg_c = total[0:1] / coarse_count
    inv_c = lax.rsqrt(total[1:2] / coarse_count - avg_c * avg_c + EPSILON)
    gain2 = gain_c[...]
    inside_c = (within(prow + (gy * h - 1), 0, h * ngy) & within(pcol + (gx * w - 1), 0, w * ngx))
    norm_c = (CI[...] - avg_c) * inv_c
    act = norm_c * gain2
    sigma = 1.0 / (1.0 + jnp.exp(-act))
    dact_c = DC[...] * (sigma * (1.0 + act * (1.0 - sigma)))
    DC[...] = dact_c
    kept = jnp.where(inner, dact_c, 0.0)
    sums_start(2, split_rows(jnp.concatenate([
        jnp.sum(kept, axis=0, keepdims=True),
        jnp.sum(kept * norm_c, axis=0, keepdims=True)], axis=0)))

    HC[0:ext] = jnp.where(inside_c, act * sigma, 0.0)
    HC[ext:] = jnp.zeros((HC.shape[0] - ext, c2), F32)
    for tap in range(3):
        X3c[:, tap * c2:(tap + 1) * c2] = HC[pl.ds(tap, ext), :].astype(BF16)
    cells_c = h * wpc
    gb = grads.T.astype(BF16)
    taps_c = 3 * c2
    for a in range(3):
        part = jnp.dot(gb, X3c[a * wpc:a * wpc + cells_c, :], preferred_element_type=F32)
        part = part.T.astype(BF16)
        for half in range(2):
            at = (3 * half + a) * taps_c
            data_c[at:at + taps_c] = part[:, half * 128:(half + 1) * 128]
    if data_c.shape[0] > 6 * taps_c:
        data_c[6 * taps_c:] = jnp.zeros((data_c.shape[0] - 6 * taps_c, 128), BF16)

    core, chip = lax.rem(gx, 2), lax.div(gx, 2)
    levels = (
        ("core", 2, core, lambda k: (gy, chip * 2 + k)),
        ("chip", ngx // 2, chip, lambda k: (gy, k * 2 + core)),
        ("gy", ngy, gy, lambda k: (k, gx)),
    )
    big = Reducer(levels, data_c.shape[0], data_c, full_c, (lc1, lc2, lc3), c_send, c_recv)
    small = Reducer(levels, data_f.shape[0], data_f, full_f, (lf1, lf2, lf3), f_send, f_recv)
    big.start(0)

    out = CI[pl.ds(wpc + 1, cells_c), :]
    for a in range(3):
        out = out + jnp.dot(X3c[a * wpc:a * wpc + cells_c, :], wc[a], preferred_element_type=F32)
    cout[...] = out.reshape(h, wpc, c2)[:, :w].astype(BF16)
    stores[0].start()

    big.finish(0)
    big.start(1)

    total = joined(sums_finish(2))
    gc_grad[...] = total[1:2]
    stores[6].start()
    total = group_sums(total[0:2] * gain2, c2 // GROUPS)
    first, second = total[0:1] / coarse_count, total[1:2] / coarse_count
    norm_c = (CI[...] - avg_c) * inv_c
    dcoarse = inv_c * (DC[...] * gain2 - first - norm_c * second)
    dcoarse = dcoarse + jnp.concatenate(
        [C[0, pl.ds(wpc + 1, ext), :], C[1, pl.ds(wpc + 1, ext), :]], axis=1)
    dcoarse = jnp.where(inside_c, dcoarse, 0.0).astype(BF16)
    pgrad = matmul_tn(pooled_in, dcoarse).astype(BF16)
    taps_f = 9 * c1
    for half in range(2):
        at = taps_f + half * c1
        data_f[at:at + c1] = pgrad[:, half * 128:(half + 1) * 128]
    if data_f.shape[0] > taps_f + 2 * c1:
        data_f[taps_f + 2 * c1:] = jnp.zeros((data_f.shape[0] - taps_f - 2 * c1, 128), BF16)
    dsmall = (matmul_nt(dcoarse, proj[...]) * 0.25).astype(BF16).astype(F32)
    PU[pl.ds(0, ext, stride=2), :] = dsmall
    PU[pl.ds(1, ext, stride=2), :] = dsmall
    wide = PU[...].reshape(h + 2, 1, wp, c1)
    D[0:span] = jnp.broadcast_to(wide, (h + 2, 2, wp, c1)).reshape(span, c1)
    D[span:] = jnp.zeros((D.shape[0] - span, c1), F32)
    cells_f = H * wp
    _, col = cell_of((cells_f, c1), wp)
    gm = jnp.where(within(col, 2, W + 2), D[2 * wp:2 * wp + cells_f], 0.0).T.astype(BF16)
    for a in range(3):
        part = jnp.dot(gm, X3f[(2 + a) * wp:(2 + a) * wp + cells_f, :], preferred_element_type=F32)
        data_f[a * 3 * c1:(a + 1) * 3 * c1] = part.T.astype(BF16)
    small.start(0)
    big.finish(1)
    big.start(2)
    for tap in range(3):
        X3d[:, tap * c1:(tap + 1) * c1] = D[pl.ds(tap, span), :].astype(BF16)
    dact = jnp.zeros((cells_f, c1), F32)
    for a in range(3):
        for b in range(3):
            dact = dact + matmul_nt(X3d[(1 + a) * wp:(1 + a) * wp + cells_f, b * c1:(b + 1) * c1],
                                    wf[2 - a, (2 - b) * c1:(3 - b) * c1, :])
    norm_f = (E[pl.ds(3 * wp + 2, cells_f), :] - avg_f) * inv_f
    act = norm_f * gain
    sigma = 1.0 / (1.0 + jnp.exp(-act))
    dact = dact * (sigma * (1.0 + act * (1.0 - sigma)))
    kept = jnp.where(within(col, 1, W + 1), dact, 0.0)
    sums_start(3, jnp.concatenate([
        jnp.sum(kept, axis=0, keepdims=True),
        jnp.sum(kept * norm_f, axis=0, keepdims=True)], axis=0))
    T[0:cells_f] = dact

    small.finish(0)
    small.start(1)
    big.finish(2)
    big.start(3)

    total = sums_finish(3)[0:2]
    big.finish(3)
    big.start(4)
    small.finish(1)
    small.start(2)
    gf_grad[...] = total[1:2]
    stores[3].start()
    total = group_sums(total * gain, c1 // GROUPS)
    first, second = total[0:1] / fine_count, total[1:2] / fine_count
    norm_f = (E[pl.ds(3 * wp + 2, cells_f), :] - avg_f) * inv_f
    result = inv_f * (T[0:cells_f] * gain - first - norm_f * second)
    T[0:cells_f] = result + D[pl.ds(2 * wp + 1, cells_f), :]
    T[cells_f:] = jnp.zeros((T.shape[0] - cells_f, c1), F32)
    fgrad[...] = T[pl.ds(1, cells_f), :].reshape(H, wp, c1)[:, :W].astype(BF16)
    stores[1].start()

    small.finish(2)
    small.start(3)
    small.finish(3)
    small.start(4)
    big.finish(4)
    big.start(5)
    small.finish(4)
    small.start(5)
    big.finish(5)
    for half in range(2):
        at = 3 * half * taps_c
        wc_grad[:, half * 128:(half + 1) * 128] = full_c[at:at + 3 * taps_c]
    stores[5].start()
    small.finish(5)
    wf_grad[...] = full_f[0:taps_f]
    stores[2].start()
    for half in range(2):
        at = taps_f + half * c1
        proj_grad[:, half * 128:(half + 1) * 128] = full_f[at:at + c1]
    stores[4].start()
    for copy in stores:
        copy.wait()

    for number, (dy, dx) in enumerate(DIRS):
        @pl.when(reaches(dy, dx))
        def _():
            rim_copy(number).wait_send()


def deliver(cout, fgrad, wf_grad, gf_grad, proj_grad, wc_grad, gc_grad, *rest):
    outs, held, wide, load_sem, store_sem = rest[:7], rest[7:14], rest[14:17], rest[17], rest[18]
    sources = (cout, fgrad, wf_grad, gf_grad, proj_grad, wc_grad, gc_grad)
    ready = list(held)
    ready[5], ready[2], ready[4] = wide
    order = (5, 2, 4, 1, 0, 3, 6)
    loads = [pltpu.make_async_copy(sources[k], held[k], load_sem.at[k]) for k in range(7)]
    stores = [pltpu.make_async_copy(ready[k], outs[k], store_sem.at[k]) for k in range(7)]
    for k in order:
        loads[k].start()
    for k in order:
        loads[k].wait()
        if ready[k] is not held[k]:
            ready[k][...] = held[k][...].astype(F32)
        stores[k].start()
    for k in order:
        stores[k].wait()


def on_device(field, cotangent, gain_fine, weight_fine, projection, gain_coarse, weight_coarse):
    H, W, c1 = field.shape
    h, w, c2 = cotangent.shape
    ngy, ngx = lax.axis_size("gy"), lax.axis_size("gx")
    everyone = ngy * ngx
    wpc = round_up(w + 4, 16)
    wp = 2 * wpc
    sizes = (H, W, h, w, wp, wpc, ngy, ngx)
    rows_c = everyone * round_up(-(-18 * c2 // everyone), 16)
    rows_f = everyone * round_up(-(-11 * c1 // everyone), 16)
    counts = (2, ngx // 2, ngy)
    most = max(counts)

    def landings(rows):
        out = []
        for count in counts:
            rows //= count
            out.append(pltpu.VMEM((count, rows, 128), BF16))
        return out

    DMA = pltpu.SemaphoreType.DMA
    scratch = [
        pltpu.VMEM((H, W, c1), BF16),
        pltpu.VMEM((h, w, c2), BF16),
        pltpu.VMEM((1, c1), F32),
        pltpu.VMEM((3, 3 * c1, c1), BF16),
        pltpu.VMEM((c1, c2), BF16),
        pltpu.VMEM((1, c2), F32),
        pltpu.VMEM((3, 3 * c2, c2), BF16),
        DMA((7,)),
        pltpu.VMEM(((H + 8) * wp, c1), F32),
        pltpu.VMEM(((H + 8) * wp, c1), F32),
        pltpu.VMEM(((H + 6) * wp, 3 * c1), BF16),
        pltpu.VMEM(((h + 2) * wp, c1), F32),
        pltpu.VMEM(((h + 2) * wpc, c2), F32),
        pltpu.VMEM(((h + 4) * wpc, c2), F32),
        pltpu.VMEM(((h + 2) * wpc, 3 * c2), BF16),
        pltpu.VMEM((2, (h + 6) * wpc, 128), F32),
        pltpu.VMEM(((h + 4) * wpc, 3 * c2), BF16),
        pltpu.VMEM(((h + 2) * wpc, c2), F32),
        pltpu.VMEM(((H + 6) * wp, c1), F32),
        pltpu.VMEM(((H + 4) * wp, 3 * c1), BF16),
        pltpu.VMEM(((H + 1) * wp, c1), F32),
        pltpu.VMEM((2, 3 * wp + 4 * wpc, 128), BF16),
        pltpu.VMEM((2, 3 * H + 4 * h, 128), BF16),
        pltpu.VMEM((8, 3 * wp + 4 * wpc, 128), BF16),
        pltpu.VMEM((2, 3 * H + 4 * h, 128), BF16),
        pltpu.VMEM((4, everyone, 8, 128), F32),
        pltpu.VMEM((rows_c, 128), BF16), pltpu.VMEM((rows_c, 128), BF16), *landings(rows_c),
        pltpu.VMEM((rows_f, 128), BF16), pltpu.VMEM((rows_f, 128), BF16), *landings(rows_f),
        DMA((8,)), DMA((8,)),
        DMA((everyone,)), DMA((2, everyone)),
        DMA((6, most)), DMA((6, most)),
        DMA((6, most)), DMA((6, most)),
    ]
    def shapes(kind):
        return (
            jax.ShapeDtypeStruct((h, w, c2), BF16),
            jax.ShapeDtypeStruct((H, W, c1), BF16),
            jax.ShapeDtypeStruct((9 * c1, c1), kind),
            jax.ShapeDtypeStruct((1, c1), F32),
            jax.ShapeDtypeStruct((c1, c2), kind),
            jax.ShapeDtypeStruct((9 * c2, c2), kind),
            jax.ShapeDtypeStruct((1, c2), F32),
        )

    hbm = pl.BlockSpec(memory_space=pltpu.HBM)
    results = pl.pallas_call(
        functools.partial(kernel, sizes),
        out_shape=shapes(BF16),
        in_specs=[hbm] * 7,
        out_specs=[hbm] * 7,
        scratch_shapes=[pltpu.VMEM(shape.shape, shape.dtype) for shape in shapes(BF16)]
        + [DMA((7,))] + scratch,
        compiler_params=pltpu.CompilerParams(
            collective_id=0, has_side_effects=True, vmem_limit_bytes=63 * 2**20),
    )(
        field, cotangent, gain_fine.reshape(1, c1), weight_fine.reshape(3, 3 * c1, c1),
        projection, gain_coarse.reshape(1, c2), weight_coarse.reshape(3, 3 * c2, c2),
    )
    cout, fgrad, wf_grad, gf_grad, proj_grad, wc_grad, gc_grad = pl.pallas_call(
        deliver,
        out_shape=shapes(F32),
        in_specs=[hbm] * 7,
        out_specs=[hbm] * 7,
        scratch_shapes=[pltpu.VMEM(shape.shape, shape.dtype) for shape in shapes(BF16)] + [
            pltpu.VMEM((9 * c2, c2), F32), pltpu.VMEM((9 * c1, c1), F32),
            pltpu.VMEM((c1, c2), F32), DMA((7,)), DMA((7,)),
        ],
        compiler_params=pltpu.CompilerParams(vmem_limit_bytes=63 * 2**20),
    )(*results)
    return (
        cout, fgrad, wf_grad.reshape(3, 3, c1, c1), gf_grad.reshape(c1), proj_grad,
        wc_grad.reshape(3, 3, c2, c2), gc_grad.reshape(c2),
    )


def solution(mesh):
    return jax.shard_map(
        on_device,
        mesh=mesh,
        in_specs=(P("gy", "gx", None), P("gy", "gx", None), P(), P(), P(), P(), P()),
        out_specs=(P("gy", "gx", None), P("gy", "gx", None), P(), P(), P(), P(), P()),
        check_vma=False,
    )
```

```python
import functools

import jax
import jax.numpy as jnp
from jax import lax
from jax.experimental import pallas as pl
from jax.experimental.pallas import tpu as pltpu
from jax.sharding import PartitionSpec as P

GROUPS = 32
EPSILON = 1e-05
F32 = jnp.float32
BF16 = jnp.bfloat16
MESH = pl.DeviceIdType.MESH
DIRS = ((1, 0), (-1, 0), (0, 1), (0, -1), (1, 1), (1, -1), (-1, 1), (-1, -1))


def round_up(value, unit):
    return -(-value // unit) * unit


def log2(value):
    assert value & (value - 1) == 0
    return value.bit_length() - 1


def cell_of(shape, pitch):
    index = lax.broadcasted_iota(jnp.int32, shape, 0)
    return lax.shift_right_logical(index, log2(pitch)), index & (pitch - 1)


def within(value, low, high):
    return (value >= low) & (value < high)


def group_sums(sums, per_group):
    channels = sums.shape[1]
    bits = log2(per_group)
    one = lax.broadcasted_iota(jnp.int32, (channels, channels), 0)
    two = lax.broadcasted_iota(jnp.int32, (channels, channels), 1)
    same = lax.shift_right_logical(one, bits) == lax.shift_right_logical(two, bits)
    high = sums.astype(BF16)
    rest = sums - high.astype(F32)
    middle = rest.astype(BF16)
    low = (rest - middle.astype(F32)).astype(BF16)
    count = sums.shape[0]
    pad = jnp.zeros((16 - 3 * count, channels), F32)
    parts = jnp.concatenate(
        [high.astype(F32), middle.astype(F32), low.astype(F32), pad], axis=0).astype(BF16)
    total = jnp.dot(parts, same.astype(F32).astype(BF16), preferred_element_type=F32)
    return total[0:count] + total[count:2 * count] + total[2 * count:3 * count]


def sigmoid(act):
    return 0.5 + 0.5 * jnp.tanh(0.5 * act)


def fold(values):
    return jnp.sum(values.reshape(-1, 8, values.shape[1]), axis=0)


def unfold(partial):
    return jnp.sum(partial, axis=0, keepdims=True)


def matmul_nt(left, right):
    return lax.dot_general(left, right, (((1,), (1,)), ((), ())), preferred_element_type=F32)


def matmul_tn(left, right):
    return lax.dot_general(left, right, (((0,), (0,)), ((), ())), preferred_element_type=F32)


def split_rows(sums):
    return jnp.concatenate([sums[:, :128], sums[:, 128:]], axis=0)


class Reducer:
    def __init__(self, levels, rows, data, full, landings, sends, recvs):
        self.levels, self.rows = levels, rows
        self.data, self.full, self.landings = data, full, landings
        self.sends, self.recvs = sends, recvs

    def span(self, base, count):
        return pl.ds(pl.multiple_of(base, 16), count)

    def offset(self, depth):
        base, size = 0, self.rows
        for _, count, index, _ in self.levels[:depth]:
            size //= count
            base = base + index * size
        return base, size

    def copies(self, stage):
        depth = len(self.levels)
        gather = stage >= depth
        level = 2 * depth - 1 - stage if gather else stage
        _, count, index, device = self.levels[level]
        base, size = self.offset(level)
        part = size // count
        out = []
        for step in range(1, count):
            peer = lax.rem(index + step, count)
            if gather:
                own = self.full.at[self.span(base + index * part, part)]
                src, dst, theirs = own, own, self.full.at[self.span(base + peer * part, part)]
            else:
                src = self.data.at[self.span(base + peer * part, part)]
                dst = self.landings[level].at[index]
                theirs = self.landings[level].at[peer]
            out.append((
                pltpu.make_async_remote_copy(
                    src_ref=src, dst_ref=dst,
                    send_sem=self.sends.at[stage, step], recv_sem=self.recvs.at[stage, index],
                    device_id=device(peer), device_id_type=MESH,
                ),
                pltpu.make_async_remote_copy(
                    src_ref=theirs, dst_ref=theirs,
                    send_sem=self.sends.at[stage, step], recv_sem=self.recvs.at[stage, peer],
                    device_id=device(peer), device_id_type=MESH,
                ),
            ))
        return out

    def start(self, stage):
        for copy, _ in self.copies(stage):
            copy.start()

    def finish(self, stage):
        depth = len(self.levels)
        for copy, arrival in self.copies(stage):
            copy.wait_send()
            arrival.wait_recv()
        if stage < depth:
            _, count, index, _ = self.levels[stage]
            base, size = self.offset(stage)
            part = size // count
            mine = self.span(base + index * part, part)
            landing = self.landings[stage]
            landing[index] = self.data[mine]
            total = landing[0].astype(F32)
            for source in range(1, count):
                total = total + landing[source].astype(F32)
            target = self.full if stage == depth - 1 else self.data
            target[mine] = total.astype(BF16)


class Pair:
    def __init__(self, *members):
        self.members = members

    def start(self, stage):
        for member in self.members:
            member.start(stage)

    def finish(self, stage):
        for member in self.members:
            member.finish(stage)


def kernel(sizes, field_h, cot_h, gain_f_h, wf_h, proj_h, gain_c_h, wc_h,
           cout_h, fgrad_h, wf_grad_h, gf_grad_h, proj_grad_h, wc_grad_h, gc_grad_h,
           cout, fgrad, wf_grad, gf_grad, proj_grad, wc_grad, gc_grad, store_sem,
           field, cot, gain_f, wf, proj, gain_c, wc, load_sem,
           E, HF, X3f, PU, CI, HC, X3c, C, X3g, DC, D, X3d, T,
           row_out, col_out, row_in, col_in, slots,
           data_c, full_c, lc1, lc2, lc3, data_b, full_b, lb1, lb2, lb3, data_f, full_f, lf1, lf2, lf3,
           rim_send, rim_recv, sum_send, sum_recv, c_send, c_recv, b_send, b_recv, f_send, f_recv):
    H, W, h, w, wp, wpc, ngy, ngx = sizes
    c1, c2 = proj.shape
    count_all = ngy * ngx
    gy, gx = lax.axis_index("gy"), lax.axis_index("gx")
    me = gy * ngx + gx
    fine_count = float(H * W * count_all * (c1 // GROUPS))
    coarse_count = float(h * w * count_all * (c2 // GROUPS))

    def wrapped(place, count):
        return jnp.where(place >= count, place - count, place)

    few = count_all <= 64
    if few:
        rows_of = [wrapped(gy + dy, ngy) for dy in range(ngy)]
        cols_of = [wrapped(gx + dx, ngx) for dx in range(ngx)]

    def peer_of(step):
        if few:
            place = (rows_of[step // ngx], cols_of[step % ngx])
            return place[0] * ngx + place[1], place
        peer = lax.rem(me + step, count_all)
        return peer, (lax.div(peer, ngx), lax.rem(peer, ngx))

    def each_peer(body):
        if few:
            for step in range(1, count_all):
                body(step)
        else:
            pl.loop(1, count_all)(body)

    loads = [
        pltpu.make_async_copy(src, dst, load_sem.at[number])
        for number, (src, dst) in enumerate(zip(
            (field_h, cot_h, gain_f_h, wf_h, proj_h, gain_c_h, wc_h),
            (field, cot, gain_f, wf, proj, gain_c, wc)))
    ]
    for number in (0, 1, 6, 2, 3, 4, 5):
        loads[number].start()
    stores = [
        pltpu.make_async_copy(src, dst, store_sem.at[number])
        for number, (src, dst) in enumerate(zip(
            (cout, fgrad, wf_grad, gf_grad, proj_grad, wc_grad, gc_grad),
            (cout_h, fgrad_h, wf_grad_h, gf_grad_h, proj_grad_h, wc_grad_h, gc_grad_h)))
    ]
    barrier = pltpu.get_barrier_semaphore()

    def greet(step):
        pl.semaphore_signal(barrier, inc=1, device_id=peer_of(step)[1], device_id_type=MESH)

    each_peer(greet)

    def sum_copy(turn, step):
        peer, device = peer_of(step)
        go = pltpu.make_async_remote_copy(
            src_ref=slots.at[turn, me], dst_ref=slots.at[turn, me],
            send_sem=sum_send.at[step], recv_sem=sum_recv.at[turn % 2, me],
            device_id=device, device_id_type=MESH)
        come = pltpu.make_async_remote_copy(
            src_ref=slots.at[turn, peer], dst_ref=slots.at[turn, peer],
            send_sem=sum_send.at[step], recv_sem=sum_recv.at[turn % 2, peer],
            device_id=device, device_id_type=MESH)
        return go, come

    def sums_start(turn, rows):
        pad = jnp.zeros((8 - rows.shape[0], 128), F32)
        slots[turn, me] = jnp.concatenate([rows, pad], axis=0)

        each_peer(lambda step: sum_copy(turn, step)[0].start())

    def sums_finish(turn):
        def settle(step):
            go, come = sum_copy(turn, step)
            go.wait_send()
            come.wait_recv()

        each_peer(settle)
        return jnp.sum(slots[turn], axis=0)

    loads[0].wait()
    values = field[...].astype(F32)
    sums_f = jnp.concatenate([
        jnp.sum(values, axis=(0, 1), keepdims=True).reshape(1, c1),
        jnp.sum(values * values, axis=(0, 1), keepdims=True).reshape(1, c1)], axis=0)
    E[...] = jnp.zeros(E.shape, F32)
    E[pl.ds(3 * wp + 3, H * wp), :] = jnp.concatenate(
        [values, jnp.zeros((H, wp - W, c1), F32)], axis=1).reshape(H * wp, c1)
    loads[1].wait()
    grads = jnp.concatenate([cot[...].astype(F32), jnp.zeros((h, wpc - w, c2), F32)], axis=1)
    grads = grads.reshape(h * wpc, c2)
    C[...] = jnp.zeros(C.shape, F32)
    for half in range(2):
        C[half, pl.ds(2 * wpc + 2, h * wpc), :] = grads[:, half * 128:(half + 1) * 128]

    fr, cr = 3 * wp, 2 * wpc
    for side, (first, first_c) in enumerate(((H, h), (3, 2))):
        row_out[side, 0:fr] = E[first * wp:first * wp + fr].astype(BF16)
        for half in range(2):
            row_out[side, fr + half * cr:fr + (half + 1) * cr] = (
                C[half, first_c * wpc:first_c * wpc + cr].astype(BF16))
    for side, (first, first_c) in enumerate(((W, w), (3, 2))):
        for col in range(3):
            col_out[side, col * H:(col + 1) * H] = (
                E[pl.ds(3 * wp + first + col, H, stride=wp), :].astype(BF16))
        for half in range(2):
            for col in range(2):
                at = 3 * H + (2 * half + col) * h
                col_out[side, at:at + h] = (
                    C[half, pl.ds(2 * wpc + first_c + col, h, stride=wpc), :].astype(BF16))

    pl.semaphore_wait(barrier, count_all - 1)
    sums_start(0, sums_f)

    def rim_copy(number):
        dy, dx = DIRS[number]
        if dy != 0:
            src = row_out.at[0 if dy > 0 else 1]
            dst = row_in.at[number]
        else:
            src = col_out.at[0 if dx > 0 else 1]
            dst = col_in.at[number - 2]
        return pltpu.make_async_remote_copy(
            src_ref=src, dst_ref=dst, send_sem=rim_send.at[number], recv_sem=rim_recv.at[number],
            device_id=(gy + dy, gx + dx), device_id_type=MESH)

    def reaches(dy, dx):
        return within(gy + dy, 0, ngy) & within(gx + dx, 0, ngx)

    for number, (dy, dx) in enumerate(DIRS):
        @pl.when(reaches(dy, dx))
        def _():
            rim_copy(number).start()

    _, col_f = cell_of((fr, 128), wp)
    _, col_c = cell_of((cr, 128), wpc)

    def place(piece, dx, width, rim, cols):
        if dx == 0:
            return piece
        gap = jnp.zeros((width, 128), F32)
        if dx > 0:
            return jnp.where(cols < rim, jnp.concatenate([piece[width:], gap], axis=0), 0.0)
        moved = jnp.concatenate([gap, piece[:piece.shape[0] - width]], axis=0)
        return jnp.where(within(cols, width + rim, width + 2 * rim), moved, 0.0)

    for number, (dy, dx) in enumerate(DIRS):
        @pl.when(reaches(-dy, -dx))
        def _():
            rim_copy(number).wait_recv()
            if dy != 0:
                at = 0 if dy > 0 else (H + 3) * wp
                piece = row_in[number, 0:fr].astype(F32)
                E[at:at + fr] = E[at:at + fr] + place(piece, dx, W, 3, col_f)
                at = 0 if dy > 0 else (h + 2) * wpc
                for half in range(2):
                    piece = row_in[number, fr + half * cr:fr + (half + 1) * cr].astype(F32)
                    C[half, at:at + cr] = C[half, at:at + cr] + place(piece, dx, w, 2, col_c)
            else:
                at = 0 if dx > 0 else W + 3
                for col in range(3):
                    E[pl.ds(3 * wp + at + col, H, stride=wp), :] = (
                        col_in[number - 2, col * H:(col + 1) * H].astype(F32))
                at = 0 if dx > 0 else w + 2
                for half in range(2):
                    for col in range(2):
                        row = 3 * H + (2 * half + col) * h
                        C[half, pl.ds(2 * wpc + at + col, h, stride=wpc), :] = (
                            col_in[number - 2, row:row + h].astype(F32))

    ext = (h + 2) * wpc
    for tap in range(3):
        for half in range(2):
            at = tap * c2 + half * 128
            for go in range(0, (h + 4) * wpc, 4 * wpc):
                X3g[go:go + 4 * wpc, at:at + 128] = (
                    C[half, pl.ds(tap + go, 4 * wpc), :].astype(BF16))
    loads[6].wait()
    cells = jnp.concatenate([X3g[a * wpc:a * wpc + ext, :] for a in range(3)], axis=1)
    taps = jnp.concatenate(
        [wc[2 - a, (2 - b) * c2:(3 - b) * c2, :] for a in range(3) for b in range(3)], axis=1)
    DC[...] = matmul_nt(cells, taps)

    for number in (2, 3, 4, 5):
        loads[number].wait()
    total = group_sums(sums_finish(0)[0:2], c1 // GROUPS)
    avg_f = total[0:1] / fine_count
    inv_f = lax.rsqrt(total[1:2] / fine_count - avg_f * avg_f + EPSILON)
    gain = gain_f[...]
    scale_f = inv_f * gain
    shift_f = -avg_f * scale_f
    row, col = cell_of((4 * wp, c1), wp)
    col_inside = within(col + (gx * W - 3), 0, W * ngx)
    for go in range(0, (H + 8) * wp, 4 * wp):
        act = E[go:go + 4 * wp] * scale_f + shift_f
        inside = col_inside & within(row + (gy * H - 3 + go // wp), 0, H * ngy)
        HF[go:go + 4 * wp] = jnp.where(inside, act * sigmoid(act), 0.0)
    for tap in range(3):
        for go in range(0, (H + 6) * wp, 2 * wp):
            X3f[go:go + 2 * wp, tap * c1:(tap + 1) * c1] = (
                HF[pl.ds(tap + go, 2 * wp), :].astype(BF16))
    span = (H + 4) * wp
    cells = jnp.concatenate([X3f[a * wp:a * wp + span, :] for a in range(3)], axis=1)
    HF[0:span] = jnp.dot(cells, wf[...].reshape(9 * c1, c1), preferred_element_type=F32)
    for go in range(0, span, 4 * wp):
        block = HF[go:go + 4 * wp] + E[pl.ds(wp + 1 + go, 4 * wp), :]
        block = block.astype(BF16).astype(F32).reshape(2, 2, wp, c1)
        PU[go // 2:go // 2 + 2 * wp] = (block[:, 0] + block[:, 1]).reshape(2 * wp, c1)
    pooled = ((PU[pl.ds(0, ext, stride=2), :] + PU[pl.ds(1, ext, stride=2), :]) * 0.25)
    prow, pcol = cell_of((ext, c1), wpc)
    inner_p = within(prow, 1, h + 1) & within(pcol, 1, w + 1)
    pooled_in = jnp.where(inner_p, pooled, 0.0).astype(BF16)
    coarse_in = jnp.dot(pooled.astype(BF16), proj[...], preferred_element_type=F32)
    coarse_in = coarse_in.astype(BF16).astype(F32)
    CI[...] = coarse_in
    step_c = 2 * wpc
    prow, pcol = cell_of((step_c, c2), wpc)
    pcol_inner = within(pcol, 1, w + 1)
    pcol_inside = within(pcol + (gx * w - 1), 0, w * ngx)

    def inner_at(go):
        return pcol_inner & within(prow + go // wpc, 1, h + 1)

    def inside_at(go):
        return pcol_inside & within(prow + (gy * h - 1 + go // wpc), 0, h * ngy)

    one, two = jnp.zeros((8, c2), F32), jnp.zeros((8, c2), F32)
    for go in range(0, ext, step_c):
        kept = jnp.where(inner_at(go), CI[go:go + step_c], 0.0)
        one, two = one + fold(kept), two + fold(kept * kept)
    sums_start(1, split_rows(jnp.concatenate([unfold(one), unfold(two)], axis=0)))

    def joined(rows):
        return jnp.concatenate([rows[0:2], rows[2:4]], axis=1)

    total = group_sums(joined(sums_finish(1)), c2 // GROUPS)
    avg_c = total[0:1] / coarse_count
    inv_c = lax.rsqrt(total[1:2] / coarse_count - avg_c * avg_c + EPSILON)
    gain2 = gain_c[...]
    one, two = jnp.zeros((8, c2), F32), jnp.zeros((8, c2), F32)
    for go in range(0, ext, step_c):
        norm_c = (CI[go:go + step_c] - avg_c) * inv_c
        act = norm_c * gain2
        sigma = sigmoid(act)
        dact_c = DC[go:go + step_c] * (sigma * (1.0 + act * (1.0 - sigma)))
        DC[go:go + step_c] = dact_c
        kept = jnp.where(inner_at(go), dact_c, 0.0)
        one, two = one + fold(kept), two + fold(kept * norm_c)
        HC[go:go + step_c] = jnp.where(inside_at(go), act * sigma, 0.0)
    sums_start(2, split_rows(jnp.concatenate([unfold(one), unfold(two)], axis=0)))
    HC[ext:] = jnp.zeros((HC.shape[0] - ext, c2), F32)
    for tap in range(3):
        for go in range(0, ext, step_c):
            X3c[go:go + step_c, tap * c2:(tap + 1) * c2] = (
                HC[pl.ds(tap + go, step_c), :].astype(BF16))
    cells_c = h * wpc
    gb = grads.T.astype(BF16)
    taps_c = 3 * c2
    for a in range(3):
        part = jnp.dot(gb, X3c[a * wpc:a * wpc + cells_c, :], preferred_element_type=F32)
        part = part.T.astype(BF16)
        target, base = (data_c, a * 2 * taps_c) if a < 2 else (data_b, 0)
        for half in range(2):
            at = base + half * taps_c
            target[at:at + taps_c] = part[:, half * 128:(half + 1) * 128]
    for target, used in ((data_c, 4 * taps_c), (data_b, 2 * taps_c)):
        if target.shape[0] > used:
            target[used:] = jnp.zeros((target.shape[0] - used, 128), BF16)

    core, chip = lax.rem(gx, 2), lax.div(gx, 2)
    levels = (
        ("core", 2, core, lambda k: (gy, chip * 2 + k)),
        ("chip", ngx // 2, chip, lambda k: (gy, k * 2 + core)),
        ("gy", ngy, gy, lambda k: (k, gx)),
    )
    turned = (levels[0], levels[2], levels[1])
    big = Pair(
        Reducer(levels, data_c.shape[0], data_c, full_c, (lc1, lc2, lc3), c_send, c_recv),
        Reducer(turned, data_b.shape[0], data_b, full_b, (lb1, lb2, lb3), b_send, b_recv))
    small = Reducer(levels, data_f.shape[0], data_f, full_f, (lf1, lf2, lf3), f_send, f_recv)
    big.start(0)

    cells = jnp.concatenate([X3c[a * wpc:a * wpc + cells_c, :] for a in range(3)], axis=1)
    HC[0:cells_c] = jnp.dot(cells, wc[...].reshape(9 * c2, c2), preferred_element_type=F32)
    for go in range(0, cells_c, step_c):
        out = HC[go:go + step_c] + CI[pl.ds(wpc + 1 + go, step_c), :]
        cout[go // wpc:go // wpc + 2] = out.reshape(2, wpc, c2)[:, :w].astype(BF16)
    stores[0].start()

    big.finish(0)
    big.start(1)

    total = joined(sums_finish(2))
    gc_grad[...] = total[1:2]
    stores[6].start()
    total = group_sums(total[0:2] * gain2, c2 // GROUPS)
    first, second = total[0:1] / coarse_count, total[1:2] / coarse_count
    scale_c = inv_c * gain2
    for go in range(0, ext, step_c):
        norm_c = (CI[go:go + step_c] - avg_c) * inv_c
        dcoarse = DC[go:go + step_c] * scale_c - inv_c * (first + norm_c * second)
        dcoarse = dcoarse + jnp.concatenate(
            [C[half, pl.ds(wpc + 1 + go, step_c), :] for half in range(2)], axis=1)
        X3g[go:go + step_c, 0:c2] = jnp.where(inside_at(go), dcoarse, 0.0).astype(BF16)
    dcoarse = X3g[0:ext, 0:c2]
    pgrad = matmul_tn(pooled_in, dcoarse).astype(BF16)
    taps_f = 9 * c1
    for half in range(2):
        at = taps_f + half * c1
        data_f[at:at + c1] = pgrad[:, half * 128:(half + 1) * 128]
    if data_f.shape[0] > taps_f + 2 * c1:
        data_f[taps_f + 2 * c1:] = jnp.zeros((data_f.shape[0] - taps_f - 2 * c1, 128), BF16)
    dsmall = (matmul_nt(dcoarse, proj[...]) * 0.25).astype(BF16).astype(F32)
    PU[pl.ds(0, ext, stride=2), :] = dsmall
    PU[pl.ds(1, ext, stride=2), :] = dsmall
    for pair in range(h + 2):
        wide = PU[pair * wp:(pair + 1) * wp]
        D[2 * pair * wp:(2 * pair + 1) * wp] = wide
        D[(2 * pair + 1) * wp:(2 * pair + 2) * wp] = wide
    D[span:] = jnp.zeros((D.shape[0] - span, c1), F32)
    cells_f = H * wp
    _, col = cell_of((cells_f, c1), wp)
    gm = jnp.where(within(col, 2, W + 2), D[2 * wp:2 * wp + cells_f], 0.0).T.astype(BF16)
    for a in range(3):
        part = jnp.dot(gm, X3f[(2 + a) * wp:(2 + a) * wp + cells_f, :], preferred_element_type=F32)
        data_f[a * 3 * c1:(a + 1) * 3 * c1] = part.T.astype(BF16)
    small.start(0)
    big.finish(1)
    big.start(2)
    for tap in range(3):
        for go in range(0, span, 4 * wp):
            X3d[go:go + 4 * wp, tap * c1:(tap + 1) * c1] = (
                D[pl.ds(tap + go, 4 * wp), :].astype(BF16))
    cells = jnp.concatenate(
        [X3d[(1 + a) * wp:(1 + a) * wp + cells_f, :] for a in range(3)], axis=1)
    taps = jnp.concatenate(
        [wf[2 - a, (2 - b) * c1:(3 - b) * c1, :] for a in range(3) for b in range(3)], axis=1)
    T[0:cells_f] = matmul_nt(cells, taps)
    _, col = cell_of((4 * wp, c1), wp)
    own_col = within(col, 1, W + 1)
    one, two = jnp.zeros((8, c1), F32), jnp.zeros((8, c1), F32)
    for go in range(0, cells_f, 4 * wp):
        norm_f = (E[pl.ds(3 * wp + 2 + go, 4 * wp), :] - avg_f) * inv_f
        act = norm_f * gain
        sigma = sigmoid(act)
        dact = T[go:go + 4 * wp] * (sigma * (1.0 + act * (1.0 - sigma)))
        T[go:go + 4 * wp] = dact
        kept = jnp.where(own_col, dact, 0.0)
        one, two = one + fold(kept), two + fold(kept * norm_f)
    sums_start(3, jnp.concatenate([unfold(one), unfold(two)], axis=0))

    small.finish(0)
    small.start(1)
    big.finish(2)
    big.start(3)

    total = sums_finish(3)[0:2]
    big.finish(3)
    big.start(4)
    small.finish(1)
    small.start(2)
    gf_grad[...] = total[1:2]
    stores[3].start()
    total = group_sums(total * gain, c1 // GROUPS)
    first, second = total[0:1] / fine_count, total[1:2] / fine_count
    T[cells_f:] = jnp.zeros((T.shape[0] - cells_f, c1), F32)
    for go in range(0, cells_f, 4 * wp):
        norm_f = (E[pl.ds(3 * wp + 2 + go, 4 * wp), :] - avg_f) * inv_f
        result = T[go:go + 4 * wp] * scale_f - inv_f * (first + norm_f * second)
        T[go:go + 4 * wp] = result + D[pl.ds(2 * wp + 1 + go, 4 * wp), :]
    for go in range(0, cells_f, 4 * wp):
        result = T[pl.ds(1 + go, 4 * wp), :].reshape(4, wp, c1)
        fgrad[go // wp:go // wp + 4] = result[:, :W].astype(BF16)
    stores[1].start()

    small.finish(2)
    small.start(3)
    small.finish(3)
    small.start(4)
    big.finish(4)
    big.start(5)
    small.finish(4)
    small.start(5)
    big.finish(5)
    for a in range(3):
        source, base = (full_c, a * 2 * taps_c) if a < 2 else (full_b, 0)
        for half in range(2):
            at = base + half * taps_c
            wc_grad[a * taps_c:(a + 1) * taps_c, half * 128:(half + 1) * 128] = (
                source[at:at + taps_c])
    stores[5].start()
    small.finish(5)
    wf_grad[...] = full_f[0:taps_f]
    stores[2].start()
    for half in range(2):
        at = taps_f + half * c1
        proj_grad[:, half * 128:(half + 1) * 128] = full_f[at:at + c1]
    stores[4].start()
    for copy in stores:
        copy.wait()

    for number, (dy, dx) in enumerate(DIRS):
        @pl.when(reaches(dy, dx))
        def _():
            rim_copy(number).wait_send()


def deliver(cout, fgrad, wf_grad, gf_grad, proj_grad, wc_grad, gc_grad, *rest):
    outs, held, wide, load_sem, store_sem = rest[:7], rest[7:14], rest[14:17], rest[17], rest[18]
    sources = (cout, fgrad, wf_grad, gf_grad, proj_grad, wc_grad, gc_grad)
    ready = list(held)
    ready[5], ready[2], ready[4] = wide
    order = (5, 2, 4, 1, 0, 3, 6)
    loads = [pltpu.make_async_copy(sources[k], held[k], load_sem.at[k]) for k in range(7)]
    stores = [pltpu.make_async_copy(ready[k], outs[k], store_sem.at[k]) for k in range(7)]
    for k in order:
        loads[k].start()
    for k in order:
        loads[k].wait()
        if ready[k] is not held[k]:
            ready[k][...] = held[k][...].astype(F32)
        stores[k].start()
    for k in order:
        stores[k].wait()


def on_device(field, cotangent, gain_fine, weight_fine, projection, gain_coarse, weight_coarse):
    H, W, c1 = field.shape
    h, w, c2 = cotangent.shape
    ngy, ngx = lax.axis_size("gy"), lax.axis_size("gx")
    everyone = ngy * ngx
    wpc = round_up(w + 4, 16)
    wp = 2 * wpc
    sizes = (H, W, h, w, wp, wpc, ngy, ngx)
    rows_c = everyone * round_up(-(-12 * c2 // everyone), 16)
    rows_b = everyone * round_up(-(-6 * c2 // everyone), 16)
    rows_f = everyone * round_up(-(-11 * c1 // everyone), 16)
    counts = (2, ngx // 2, ngy)
    most = max(counts)

    def landings(rows, order=counts):
        out = []
        for count in order:
            rows //= count
            out.append(pltpu.VMEM((count, rows, 128), BF16))
        return out

    DMA = pltpu.SemaphoreType.DMA
    scratch = [
        pltpu.VMEM((H, W, c1), BF16),
        pltpu.VMEM((h, w, c2), BF16),
        pltpu.VMEM((1, c1), F32),
        pltpu.VMEM((3, 3 * c1, c1), BF16),
        pltpu.VMEM((c1, c2), BF16),
        pltpu.VMEM((1, c2), F32),
        pltpu.VMEM((3, 3 * c2, c2), BF16),
        DMA((7,)),
        pltpu.VMEM(((H + 8) * wp, c1), F32),
        pltpu.VMEM(((H + 8) * wp, c1), F32),
        pltpu.VMEM(((H + 6) * wp, 3 * c1), BF16),
        pltpu.VMEM(((h + 2) * wp, c1), F32),
        pltpu.VMEM(((h + 2) * wpc, c2), F32),
        pltpu.VMEM(((h + 4) * wpc, c2), F32),
        pltpu.VMEM(((h + 2) * wpc, 3 * c2), BF16),
        pltpu.VMEM((2, (h + 6) * wpc, 128), F32),
        pltpu.VMEM(((h + 4) * wpc, 3 * c2), BF16),
        pltpu.VMEM(((h + 2) * wpc, c2), F32),
        pltpu.VMEM(((H + 6) * wp, c1), F32),
        pltpu.VMEM(((H + 4) * wp, 3 * c1), BF16),
        pltpu.VMEM(((H + 1) * wp, c1), F32),
        pltpu.VMEM((2, 3 * wp + 4 * wpc, 128), BF16),
        pltpu.VMEM((2, 3 * H + 4 * h, 128), BF16),
        pltpu.VMEM((8, 3 * wp + 4 * wpc, 128), BF16),
        pltpu.VMEM((2, 3 * H + 4 * h, 128), BF16),
        pltpu.VMEM((4, everyone, 8, 128), F32),
        pltpu.VMEM((rows_c, 128), BF16), pltpu.VMEM((rows_c, 128), BF16), *landings(rows_c),
        pltpu.VMEM((rows_b, 128), BF16), pltpu.VMEM((rows_b, 128), BF16),
        *landings(rows_b, (2, ngy, ngx // 2)),
        pltpu.VMEM((rows_f, 128), BF16), pltpu.VMEM((rows_f, 128), BF16), *landings(rows_f),
        DMA((8,)), DMA((8,)),
        DMA((everyone,)), DMA((2, everyone)),
        *[DMA((6, most))] * 6,
    ]
    def shapes(kind):
        return (
            jax.ShapeDtypeStruct((h, w, c2), BF16),
            jax.ShapeDtypeStruct((H, W, c1), BF16),
            jax.ShapeDtypeStruct((9 * c1, c1), kind),
            jax.ShapeDtypeStruct((1, c1), F32),
            jax.ShapeDtypeStruct((c1, c2), kind),
            jax.ShapeDtypeStruct((9 * c2, c2), kind),
            jax.ShapeDtypeStruct((1, c2), F32),
        )

    hbm = pl.BlockSpec(memory_space=pltpu.HBM)
    results = pl.pallas_call(
        functools.partial(kernel, sizes),
        out_shape=shapes(BF16),
        in_specs=[hbm] * 7,
        out_specs=[hbm] * 7,
        scratch_shapes=[pltpu.VMEM(shape.shape, shape.dtype) for shape in shapes(BF16)]
        + [DMA((7,))] + scratch,
        compiler_params=pltpu.CompilerParams(
            collective_id=0, has_side_effects=True, vmem_limit_bytes=63 * 2**20),
    )(
        field, cotangent, gain_fine.reshape(1, c1), weight_fine.reshape(3, 3 * c1, c1),
        projection, gain_coarse.reshape(1, c2), weight_coarse.reshape(3, 3 * c2, c2),
    )
    cout, fgrad, wf_grad, gf_grad, proj_grad, wc_grad, gc_grad = pl.pallas_call(
        deliver,
        out_shape=shapes(F32),
        in_specs=[hbm] * 7,
        out_specs=[hbm] * 7,
        scratch_shapes=[pltpu.VMEM(shape.shape, shape.dtype) for shape in shapes(BF16)] + [
            pltpu.VMEM((9 * c2, c2), F32), pltpu.VMEM((9 * c1, c1), F32),
            pltpu.VMEM((c1, c2), F32), DMA((7,)), DMA((7,)),
        ],
        compiler_params=pltpu.CompilerParams(vmem_limit_bytes=63 * 2**20),
    )(*results)
    return (
        cout, fgrad, wf_grad.reshape(3, 3, c1, c1), gf_grad.reshape(c1), proj_grad,
        wc_grad.reshape(3, 3, c2, c2), gc_grad.reshape(c2),
    )


def solution(mesh):
    return jax.shard_map(
        on_device,
        mesh=mesh,
        in_specs=(P("gy", "gx", None), P("gy", "gx", None), P(), P(), P(), P(), P()),
        out_specs=(P("gy", "gx", None), P("gy", "gx", None), P(), P(), P(), P(), P()),
        check_vma=False,
    )
```

```python
import functools

import jax
import jax.numpy as jnp
from jax import lax
from jax.experimental import pallas as pl
from jax.experimental.pallas import tpu as pltpu
from jax.sharding import PartitionSpec as P

GROUPS = 32
EPSILON = 1e-05
F32 = jnp.float32
BF16 = jnp.bfloat16
MESH = pl.DeviceIdType.MESH
DIRS = ((1, 0), (-1, 0), (0, 1), (0, -1), (1, 1), (1, -1), (-1, 1), (-1, -1))


def round_up(value, unit):
    return -(-value // unit) * unit


def log2(value):
    assert value & (value - 1) == 0
    return value.bit_length() - 1


def cell_of(shape, pitch):
    index = lax.broadcasted_iota(jnp.int32, shape, 0)
    return lax.shift_right_logical(index, log2(pitch)), index & (pitch - 1)


def within(value, low, high):
    return (value >= low) & (value < high)


def group_sums(sums, per_group):
    channels = sums.shape[1]
    bits = log2(per_group)
    one = lax.broadcasted_iota(jnp.int32, (channels, channels), 0)
    two = lax.broadcasted_iota(jnp.int32, (channels, channels), 1)
    same = lax.shift_right_logical(one, bits) == lax.shift_right_logical(two, bits)
    high = sums.astype(BF16)
    rest = sums - high.astype(F32)
    middle = rest.astype(BF16)
    low = (rest - middle.astype(F32)).astype(BF16)
    count = sums.shape[0]
    pad = jnp.zeros((16 - 3 * count, channels), F32)
    parts = jnp.concatenate(
        [high.astype(F32), middle.astype(F32), low.astype(F32), pad], axis=0).astype(BF16)
    total = jnp.dot(parts, same.astype(F32).astype(BF16), preferred_element_type=F32)
    return total[0:count] + total[count:2 * count] + total[2 * count:3 * count]


def sigmoid(act):
    return 0.5 + 0.5 * jnp.tanh(0.5 * act)


def fold(values):
    return jnp.sum(values.reshape(-1, 8, values.shape[1]), axis=0)


def unfold(partial):
    return jnp.sum(partial, axis=0, keepdims=True)


def matmul_nt(left, right):
    return lax.dot_general(left, right, (((1,), (1,)), ((), ())), preferred_element_type=F32)


def matmul_tn(left, right):
    return lax.dot_general(left, right, (((0,), (0,)), ((), ())), preferred_element_type=F32)


def split_rows(sums):
    return jnp.concatenate([sums[:, :128], sums[:, 128:]], axis=0)


class Reducer:
    def __init__(self, levels, rows, data, full, landings, sends, recvs):
        self.levels, self.rows = levels, rows
        self.data, self.full, self.landings = data, full, landings
        self.sends, self.recvs = sends, recvs

    def span(self, base, count):
        return pl.ds(pl.multiple_of(base, 16), count)

    def offset(self, depth):
        base, size = 0, self.rows
        for _, count, index, _ in self.levels[:depth]:
            size //= count
            base = base + index * size
        return base, size

    def copies(self, stage):
        depth = len(self.levels)
        gather = stage >= depth
        level = 2 * depth - 1 - stage if gather else stage
        _, count, index, device = self.levels[level]
        base, size = self.offset(level)
        part = size // count
        out = []
        for step in range(1, count):
            peer = lax.rem(index + step, count)
            if gather:
                own = self.full.at[self.span(base + index * part, part)]
                src, dst, theirs = own, own, self.full.at[self.span(base + peer * part, part)]
            else:
                src = self.data.at[self.span(base + peer * part, part)]
                dst = self.landings[level].at[index]
                theirs = self.landings[level].at[peer]
            out.append((
                pltpu.make_async_remote_copy(
                    src_ref=src, dst_ref=dst,
                    send_sem=self.sends.at[stage, step], recv_sem=self.recvs.at[stage, index],
                    device_id=device(peer), device_id_type=MESH,
                ),
                pltpu.make_async_remote_copy(
                    src_ref=theirs, dst_ref=theirs,
                    send_sem=self.sends.at[stage, step], recv_sem=self.recvs.at[stage, peer],
                    device_id=device(peer), device_id_type=MESH,
                ),
            ))
        return out

    def start(self, stage):
        for copy, _ in self.copies(stage):
            copy.start()

    def finish(self, stage):
        depth = len(self.levels)
        for copy, arrival in self.copies(stage):
            copy.wait_send()
            arrival.wait_recv()
        if stage < depth:
            _, count, index, _ = self.levels[stage]
            base, size = self.offset(stage)
            part = size // count
            mine = self.span(base + index * part, part)
            landing = self.landings[stage]
            landing[index] = self.data[mine]
            total = landing[0].astype(F32)
            for source in range(1, count):
                total = total + landing[source].astype(F32)
            target = self.full if stage == depth - 1 else self.data
            target[mine] = total.astype(BF16)


class Pair:
    def __init__(self, *members):
        self.members = members

    def start(self, stage):
        for member in self.members:
            member.start(stage)

    def finish(self, stage):
        for member in self.members:
            member.finish(stage)


def kernel(sizes, field_h, cot_h, gain_f_h, wf_h, proj_h, gain_c_h, wc_h,
           cout_h, fgrad_h, wf_grad_h, gf_grad_h, proj_grad_h, wc_grad_h, gc_grad_h,
           cout, fgrad, wf_grad, gf_grad, proj_grad, wc_grad, gc_grad, store_sem,
           field, cot, gain_f, wf, proj, gain_c, wc, load_sem,
           E, HF, X3f, PU, CI, HC, X3c, C, X3g, DC, D, X3d, T,
           row_out, col_out, row_in, col_in, gx_f, gx_c, gy_f, gy_c,
           data_c, full_c, lc1, lc2, lc3, data_b, full_b, lb1, lb2, lb3, data_f, full_f, lf1, lf2, lf3,
           rim_send, rim_recv, sum_0, sum_1, sum_2, sum_3, c_send, c_recv, b_send, b_recv, f_send, f_recv):
    H, W, h, w, wp, wpc, ngy, ngx = sizes
    sum_sems = (sum_0, sum_1, sum_2, sum_3)
    c1, c2 = proj.shape
    count_all = ngy * ngx
    gy, gx = lax.axis_index("gy"), lax.axis_index("gx")
    fine_count = float(H * W * count_all * (c1 // GROUPS))
    coarse_count = float(h * w * count_all * (c2 // GROUPS))

    def wrapped(place, count):
        return jnp.where(place >= count, place - count, place)

    loads = [
        pltpu.make_async_copy(src, dst, load_sem.at[number])
        for number, (src, dst) in enumerate(zip(
            (field_h, cot_h, gain_f_h, wf_h, proj_h, gain_c_h, wc_h),
            (field, cot, gain_f, wf, proj, gain_c, wc)))
    ]
    for number in (0, 1, 6, 2, 3, 4, 5):
        loads[number].start()
    stores = [
        pltpu.make_async_copy(src, dst, store_sem.at[number])
        for number, (src, dst) in enumerate(zip(
            (cout, fgrad, wf_grad, gf_grad, proj_grad, wc_grad, gc_grad),
            (cout_h, fgrad_h, wf_grad_h, gf_grad_h, proj_grad_h, wc_grad_h, gc_grad_h)))
    ]
    barrier = pltpu.get_barrier_semaphore()

    def reaches(dy, dx):
        return within(gy + dy, 0, ngy) & within(gx + dx, 0, ngx)

    greeted = ngx - 1 + ngy - 1
    for step in range(1, ngx):
        pl.semaphore_signal(barrier, inc=1, device_id=(gy, wrapped(gx + step, ngx)),
                            device_id_type=MESH)
    for step in range(1, ngy):
        pl.semaphore_signal(barrier, inc=1, device_id=(wrapped(gy + step, ngy), gx),
                            device_id_type=MESH)
    for dy, dx in DIRS[4:]:
        there = reaches(dy, dx)
        greeted = greeted + jnp.where(there, 1, 0)

        @pl.when(there)
        def _():
            pl.semaphore_signal(barrier, inc=1, device_id=(gy + dy, gx + dx),
                                device_id_type=MESH)

    def sum_copies(turn, level):
        count, index = ((ngx, gx), (ngy, gy))[level]
        home = ((gx_f, gx_c), (gy_f, gy_c))[level][turn in (1, 2)].at[turn // 2]
        sends, recvs = sum_sems[2 * level], sum_sems[2 * level + 1]
        out = []
        for step in range(1, count):
            peer = wrapped(index + step, count)
            device = (peer, gx) if level else (gy, peer)
            out.append([
                pltpu.make_async_remote_copy(
                    src_ref=home.at[place], dst_ref=home.at[place],
                    send_sem=sends.at[turn, step], recv_sem=recvs.at[turn, place],
                    device_id=device, device_id_type=MESH)
                for place in (index, peer)
            ])
        return home, index, out

    def sums_send(turn, level, rows):
        home, index, copies = sum_copies(turn, level)
        home[index] = rows
        for go, _ in copies:
            go.start()

    def sums_take(turn, level):
        home, _, copies = sum_copies(turn, level)
        for go, come in copies:
            go.wait_send()
            come.wait_recv()
        return jnp.sum(home[...], axis=0)

    def sums_start(turn, rows):
        sums_send(turn, 0, rows)

    def sums_middle(turn):
        sums_send(turn, 1, sums_take(turn, 0))

    def sums_finish(turn):
        return sums_take(turn, 1)

    loads[0].wait()
    values = field[...].astype(F32)
    sums_f = jnp.concatenate([
        jnp.sum(values, axis=(0, 1), keepdims=True).reshape(1, c1),
        jnp.sum(values * values, axis=(0, 1), keepdims=True).reshape(1, c1)], axis=0)
    E[...] = jnp.zeros(E.shape, F32)
    E[pl.ds(3 * wp + 3, H * wp), :] = jnp.concatenate(
        [values, jnp.zeros((H, wp - W, c1), F32)], axis=1).reshape(H * wp, c1)
    loads[1].wait()
    grads = jnp.concatenate([cot[...].astype(F32), jnp.zeros((h, wpc - w, c2), F32)], axis=1)
    grads = grads.reshape(h * wpc, c2)
    C[...] = jnp.zeros(C.shape, F32)
    for half in range(2):
        C[half, pl.ds(2 * wpc + 2, h * wpc), :] = grads[:, half * 128:(half + 1) * 128]

    fr, cr = 3 * wp, 2 * wpc
    for side, (first, first_c) in enumerate(((H, h), (3, 2))):
        row_out[side, 0:fr] = E[first * wp:first * wp + fr].astype(BF16)
        for half in range(2):
            row_out[side, fr + half * cr:fr + (half + 1) * cr] = (
                C[half, first_c * wpc:first_c * wpc + cr].astype(BF16))
    for side, (first, first_c) in enumerate(((W, w), (3, 2))):
        for col in range(3):
            col_out[side, col * H:(col + 1) * H] = (
                E[pl.ds(3 * wp + first + col, H, stride=wp), :].astype(BF16))
        for half in range(2):
            for col in range(2):
                at = 3 * H + (2 * half + col) * h
                col_out[side, at:at + h] = (
                    C[half, pl.ds(2 * wpc + first_c + col, h, stride=wpc), :].astype(BF16))

    pl.semaphore_wait(barrier, greeted)
    sums_start(0, sums_f)

    def rim_copy(number):
        dy, dx = DIRS[number]
        if dy != 0:
            src = row_out.at[0 if dy > 0 else 1]
            dst = row_in.at[number]
        else:
            src = col_out.at[0 if dx > 0 else 1]
            dst = col_in.at[number - 2]
        return pltpu.make_async_remote_copy(
            src_ref=src, dst_ref=dst, send_sem=rim_send.at[number], recv_sem=rim_recv.at[number],
            device_id=(gy + dy, gx + dx), device_id_type=MESH)

    for number, (dy, dx) in enumerate(DIRS):
        @pl.when(reaches(dy, dx))
        def _():
            rim_copy(number).start()

    _, col_f = cell_of((fr, 128), wp)
    _, col_c = cell_of((cr, 128), wpc)

    def place(piece, dx, width, rim, cols):
        if dx == 0:
            return piece
        gap = jnp.zeros((width, 128), F32)
        if dx > 0:
            return jnp.where(cols < rim, jnp.concatenate([piece[width:], gap], axis=0), 0.0)
        moved = jnp.concatenate([gap, piece[:piece.shape[0] - width]], axis=0)
        return jnp.where(within(cols, width + rim, width + 2 * rim), moved, 0.0)

    for number, (dy, dx) in enumerate(DIRS):
        @pl.when(reaches(-dy, -dx))
        def _():
            rim_copy(number).wait_recv()
            if dy != 0:
                at = 0 if dy > 0 else (H + 3) * wp
                piece = row_in[number, 0:fr].astype(F32)
                E[at:at + fr] = E[at:at + fr] + place(piece, dx, W, 3, col_f)
                at = 0 if dy > 0 else (h + 2) * wpc
                for half in range(2):
                    piece = row_in[number, fr + half * cr:fr + (half + 1) * cr].astype(F32)
                    C[half, at:at + cr] = C[half, at:at + cr] + place(piece, dx, w, 2, col_c)
            else:
                at = 0 if dx > 0 else W + 3
                for col in range(3):
                    E[pl.ds(3 * wp + at + col, H, stride=wp), :] = (
                        col_in[number - 2, col * H:(col + 1) * H].astype(F32))
                at = 0 if dx > 0 else w + 2
                for half in range(2):
                    for col in range(2):
                        row = 3 * H + (2 * half + col) * h
                        C[half, pl.ds(2 * wpc + at + col, h, stride=wpc), :] = (
                            col_in[number - 2, row:row + h].astype(F32))

    sums_middle(0)

    ext = (h + 2) * wpc
    for tap in range(3):
        for half in range(2):
            at = tap * c2 + half * 128
            for go in range(0, (h + 4) * wpc, 4 * wpc):
                X3g[go:go + 4 * wpc, at:at + 128] = (
                    C[half, pl.ds(tap + go, 4 * wpc), :].astype(BF16))
    loads[6].wait()
    cells = jnp.concatenate([X3g[a * wpc:a * wpc + ext, :] for a in range(3)], axis=1)
    taps = jnp.concatenate(
        [wc[2 - a, (2 - b) * c2:(3 - b) * c2, :] for a in range(3) for b in range(3)], axis=1)
    DC[...] = matmul_nt(cells, taps)

    for number in (2, 3, 4, 5):
        loads[number].wait()
    total = group_sums(sums_finish(0), c1 // GROUPS)
    avg_f = total[0:1] / fine_count
    inv_f = lax.rsqrt(total[1:2] / fine_count - avg_f * avg_f + EPSILON)
    gain = gain_f[...]
    scale_f = inv_f * gain
    shift_f = -avg_f * scale_f
    row, col = cell_of((4 * wp, c1), wp)
    col_inside = within(col + (gx * W - 3), 0, W * ngx)
    for go in range(0, (H + 8) * wp, 4 * wp):
        act = E[go:go + 4 * wp] * scale_f + shift_f
        inside = col_inside & within(row + (gy * H - 3 + go // wp), 0, H * ngy)
        HF[go:go + 4 * wp] = jnp.where(inside, act * sigmoid(act), 0.0)
    for tap in range(3):
        for go in range(0, (H + 6) * wp, 2 * wp):
            X3f[go:go + 2 * wp, tap * c1:(tap + 1) * c1] = (
                HF[pl.ds(tap + go, 2 * wp), :].astype(BF16))
    span = (H + 4) * wp
    cells = jnp.concatenate([X3f[a * wp:a * wp + span, :] for a in range(3)], axis=1)
    HF[0:span] = jnp.dot(cells, wf[...].reshape(9 * c1, c1), preferred_element_type=F32)
    for go in range(0, span, 4 * wp):
        block = HF[go:go + 4 * wp] + E[pl.ds(wp + 1 + go, 4 * wp), :]
        block = block.astype(BF16).astype(F32).reshape(2, 2, wp, c1)
        PU[go // 2:go // 2 + 2 * wp] = (block[:, 0] + block[:, 1]).reshape(2 * wp, c1)
    pooled = ((PU[pl.ds(0, ext, stride=2), :] + PU[pl.ds(1, ext, stride=2), :]) * 0.25)
    prow, pcol = cell_of((ext, c1), wpc)
    inner_p = within(prow, 1, h + 1) & within(pcol, 1, w + 1)
    pooled_in = jnp.where(inner_p, pooled, 0.0).astype(BF16)
    coarse_in = jnp.dot(pooled.astype(BF16), proj[...], preferred_element_type=F32)
    coarse_in = coarse_in.astype(BF16).astype(F32)
    CI[...] = coarse_in
    step_c = 2 * wpc
    prow, pcol = cell_of((step_c, c2), wpc)
    pcol_inner = within(pcol, 1, w + 1)
    pcol_inside = within(pcol + (gx * w - 1), 0, w * ngx)

    def inner_at(go):
        return pcol_inner & within(prow + go // wpc, 1, h + 1)

    def inside_at(go):
        return pcol_inside & within(prow + (gy * h - 1 + go // wpc), 0, h * ngy)

    one, two = jnp.zeros((8, c2), F32), jnp.zeros((8, c2), F32)
    for go in range(0, ext, step_c):
        kept = jnp.where(inner_at(go), CI[go:go + step_c], 0.0)
        one, two = one + fold(kept), two + fold(kept * kept)
    sums_start(1, split_rows(jnp.concatenate([unfold(one), unfold(two)], axis=0)))

    def joined(rows):
        return jnp.concatenate([rows[0:2], rows[2:4]], axis=1)

    sums_middle(1)
    total = group_sums(joined(sums_finish(1)), c2 // GROUPS)
    avg_c = total[0:1] / coarse_count
    inv_c = lax.rsqrt(total[1:2] / coarse_count - avg_c * avg_c + EPSILON)
    gain2 = gain_c[...]
    one, two = jnp.zeros((8, c2), F32), jnp.zeros((8, c2), F32)
    for go in range(0, ext, step_c):
        norm_c = (CI[go:go + step_c] - avg_c) * inv_c
        act = norm_c * gain2
        sigma = sigmoid(act)
        dact_c = DC[go:go + step_c] * (sigma * (1.0 + act * (1.0 - sigma)))
        DC[go:go + step_c] = dact_c
        kept = jnp.where(inner_at(go), dact_c, 0.0)
        one, two = one + fold(kept), two + fold(kept * norm_c)
        HC[go:go + step_c] = jnp.where(inside_at(go), act * sigma, 0.0)
    sums_start(2, split_rows(jnp.concatenate([unfold(one), unfold(two)], axis=0)))
    HC[ext:] = jnp.zeros((HC.shape[0] - ext, c2), F32)
    for tap in range(3):
        for go in range(0, ext, step_c):
            X3c[go:go + step_c, tap * c2:(tap + 1) * c2] = (
                HC[pl.ds(tap + go, step_c), :].astype(BF16))
    sums_middle(2)
    cells_c = h * wpc
    gb = grads.T.astype(BF16)
    taps_c = 3 * c2
    for a in range(3):
        part = jnp.dot(gb, X3c[a * wpc:a * wpc + cells_c, :], preferred_element_type=F32)
        part = part.T.astype(BF16)
        target, base = (data_c, a * 2 * taps_c) if a < 2 else (data_b, 0)
        for half in range(2):
            at = base + half * taps_c
            target[at:at + taps_c] = part[:, half * 128:(half + 1) * 128]
    for target, used in ((data_c, 4 * taps_c), (data_b, 2 * taps_c)):
        if target.shape[0] > used:
            target[used:] = jnp.zeros((target.shape[0] - used, 128), BF16)

    core, chip = lax.rem(gx, 2), lax.div(gx, 2)
    levels = (
        ("core", 2, core, lambda k: (gy, chip * 2 + k)),
        ("chip", ngx // 2, chip, lambda k: (gy, k * 2 + core)),
        ("gy", ngy, gy, lambda k: (k, gx)),
    )
    turned = (levels[0], levels[2], levels[1])
    big = Pair(
        Reducer(levels, data_c.shape[0], data_c, full_c, (lc1, lc2, lc3), c_send, c_recv),
        Reducer(turned, data_b.shape[0], data_b, full_b, (lb1, lb2, lb3), b_send, b_recv))
    small = Reducer(levels, data_f.shape[0], data_f, full_f, (lf1, lf2, lf3), f_send, f_recv)
    big.start(0)

    cells = jnp.concatenate([X3c[a * wpc:a * wpc + cells_c, :] for a in range(3)], axis=1)
    HC[0:cells_c] = jnp.dot(cells, wc[...].reshape(9 * c2, c2), preferred_element_type=F32)
    for go in range(0, cells_c, step_c):
        out = HC[go:go + step_c] + CI[pl.ds(wpc + 1 + go, step_c), :]
        cout[go // wpc:go // wpc + 2] = out.reshape(2, wpc, c2)[:, :w].astype(BF16)
    stores[0].start()

    big.finish(0)
    big.start(1)

    total = joined(sums_finish(2))
    gc_grad[...] = total[1:2]
    stores[6].start()
    total = group_sums(total[0:2] * gain2, c2 // GROUPS)
    first, second = total[0:1] / coarse_count, total[1:2] / coarse_count
    scale_c = inv_c * gain2
    for go in range(0, ext, step_c):
        norm_c = (CI[go:go + step_c] - avg_c) * inv_c
        dcoarse = DC[go:go + step_c] * scale_c - inv_c * (first + norm_c * second)
        dcoarse = dcoarse + jnp.concatenate(
            [C[half, pl.ds(wpc + 1 + go, step_c), :] for half in range(2)], axis=1)
        X3g[go:go + step_c, 0:c2] = jnp.where(inside_at(go), dcoarse, 0.0).astype(BF16)
    dcoarse = X3g[0:ext, 0:c2]
    pgrad = matmul_tn(pooled_in, dcoarse).astype(BF16)
    taps_f = 9 * c1
    for half in range(2):
        at = taps_f + half * c1
        data_f[at:at + c1] = pgrad[:, half * 128:(half + 1) * 128]
    if data_f.shape[0] > taps_f + 2 * c1:
        data_f[taps_f + 2 * c1:] = jnp.zeros((data_f.shape[0] - taps_f - 2 * c1, 128), BF16)
    dsmall = (matmul_nt(dcoarse, proj[...]) * 0.25).astype(BF16).astype(F32)
    PU[pl.ds(0, ext, stride=2), :] = dsmall
    PU[pl.ds(1, ext, stride=2), :] = dsmall
    for pair in range(h + 2):
        wide = PU[pair * wp:(pair + 1) * wp]
        D[2 * pair * wp:(2 * pair + 1) * wp] = wide
        D[(2 * pair + 1) * wp:(2 * pair + 2) * wp] = wide
    D[span:] = jnp.zeros((D.shape[0] - span, c1), F32)
    cells_f = H * wp
    _, col = cell_of((cells_f, c1), wp)
    gm = jnp.where(within(col, 2, W + 2), D[2 * wp:2 * wp + cells_f], 0.0).T.astype(BF16)
    for a in range(3):
        part = jnp.dot(gm, X3f[(2 + a) * wp:(2 + a) * wp + cells_f, :], preferred_element_type=F32)
        data_f[a * 3 * c1:(a + 1) * 3 * c1] = part.T.astype(BF16)
    small.start(0)
    big.finish(1)
    big.start(2)
    for tap in range(3):
        for go in range(0, span, 4 * wp):
            X3d[go:go + 4 * wp, tap * c1:(tap + 1) * c1] = (
                D[pl.ds(tap + go, 4 * wp), :].astype(BF16))
    cells = jnp.concatenate(
        [X3d[(1 + a) * wp:(1 + a) * wp + cells_f, :] for a in range(3)], axis=1)
    taps = jnp.concatenate(
        [wf[2 - a, (2 - b) * c1:(3 - b) * c1, :] for a in range(3) for b in range(3)], axis=1)
    T[0:cells_f] = matmul_nt(cells, taps)
    _, col = cell_of((4 * wp, c1), wp)
    own_col = within(col, 1, W + 1)
    one, two = jnp.zeros((8, c1), F32), jnp.zeros((8, c1), F32)
    for go in range(0, cells_f, 4 * wp):
        norm_f = (E[pl.ds(3 * wp + 2 + go, 4 * wp), :] - avg_f) * inv_f
        act = norm_f * gain
        sigma = sigmoid(act)
        dact = T[go:go + 4 * wp] * (sigma * (1.0 + act * (1.0 - sigma)))
        T[go:go + 4 * wp] = dact
        kept = jnp.where(own_col, dact, 0.0)
        one, two = one + fold(kept), two + fold(kept * norm_f)
    sums_start(3, jnp.concatenate([unfold(one), unfold(two)], axis=0))

    small.finish(0)
    small.start(1)
    sums_middle(3)
    big.finish(2)
    big.start(3)

    total = sums_finish(3)
    big.finish(3)
    big.start(4)
    small.finish(1)
    small.start(2)
    gf_grad[...] = total[1:2]
    stores[3].start()
    total = group_sums(total * gain, c1 // GROUPS)
    first, second = total[0:1] / fine_count, total[1:2] / fine_count
    T[cells_f:] = jnp.zeros((T.shape[0] - cells_f, c1), F32)
    for go in range(0, cells_f, 4 * wp):
        norm_f = (E[pl.ds(3 * wp + 2 + go, 4 * wp), :] - avg_f) * inv_f
        result = T[go:go + 4 * wp] * scale_f - inv_f * (first + norm_f * second)
        T[go:go + 4 * wp] = result + D[pl.ds(2 * wp + 1 + go, 4 * wp), :]
    for go in range(0, cells_f, 4 * wp):
        result = T[pl.ds(1 + go, 4 * wp), :].reshape(4, wp, c1)
        fgrad[go // wp:go // wp + 4] = result[:, :W].astype(BF16)
    stores[1].start()

    small.finish(2)
    small.start(3)
    small.finish(3)
    small.start(4)
    big.finish(4)
    big.start(5)
    small.finish(4)
    small.start(5)
    big.finish(5)
    for a in range(3):
        source, base = (full_c, a * 2 * taps_c) if a < 2 else (full_b, 0)
        for half in range(2):
            at = base + half * taps_c
            wc_grad[a * taps_c:(a + 1) * taps_c, half * 128:(half + 1) * 128] = (
                source[at:at + taps_c])
    stores[5].start()
    small.finish(5)
    wf_grad[...] = full_f[0:taps_f]
    stores[2].start()
    for half in range(2):
        at = taps_f + half * c1
        proj_grad[:, half * 128:(half + 1) * 128] = full_f[at:at + c1]
    stores[4].start()
    for copy in stores:
        copy.wait()

    for number, (dy, dx) in enumerate(DIRS):
        @pl.when(reaches(dy, dx))
        def _():
            rim_copy(number).wait_send()


def deliver(cout, fgrad, wf_grad, gf_grad, proj_grad, wc_grad, gc_grad, *rest):
    outs, held, wide, load_sem, store_sem = rest[:7], rest[7:14], rest[14:17], rest[17], rest[18]
    sources = (cout, fgrad, wf_grad, gf_grad, proj_grad, wc_grad, gc_grad)
    ready = list(held)
    ready[5], ready[2], ready[4] = wide
    order = (5, 2, 4, 1, 0, 3, 6)
    loads = [pltpu.make_async_copy(sources[k], held[k], load_sem.at[k]) for k in range(7)]
    stores = [pltpu.make_async_copy(ready[k], outs[k], store_sem.at[k]) for k in range(7)]
    for k in order:
        loads[k].start()
    for k in order:
        loads[k].wait()
        if ready[k] is not held[k]:
            ready[k][...] = held[k][...].astype(F32)
        stores[k].start()
    for k in order:
        stores[k].wait()


def on_device(field, cotangent, gain_fine, weight_fine, projection, gain_coarse, weight_coarse):
    H, W, c1 = field.shape
    h, w, c2 = cotangent.shape
    ngy, ngx = lax.axis_size("gy"), lax.axis_size("gx")
    everyone = ngy * ngx
    wpc = round_up(w + 4, 16)
    wp = 2 * wpc
    sizes = (H, W, h, w, wp, wpc, ngy, ngx)
    rows_c = everyone * round_up(-(-12 * c2 // everyone), 16)
    rows_b = everyone * round_up(-(-6 * c2 // everyone), 16)
    rows_f = everyone * round_up(-(-11 * c1 // everyone), 16)
    counts = (2, ngx // 2, ngy)
    most = max(counts)

    def landings(rows, order=counts):
        out = []
        for count in order:
            rows //= count
            out.append(pltpu.VMEM((count, rows, 128), BF16))
        return out

    DMA = pltpu.SemaphoreType.DMA
    scratch = [
        pltpu.VMEM((H, W, c1), BF16),
        pltpu.VMEM((h, w, c2), BF16),
        pltpu.VMEM((1, c1), F32),
        pltpu.VMEM((3, 3 * c1, c1), BF16),
        pltpu.VMEM((c1, c2), BF16),
        pltpu.VMEM((1, c2), F32),
        pltpu.VMEM((3, 3 * c2, c2), BF16),
        DMA((7,)),
        pltpu.VMEM(((H + 8) * wp, c1), F32),
        pltpu.VMEM(((H + 8) * wp, c1), F32),
        pltpu.VMEM(((H + 6) * wp, 3 * c1), BF16),
        pltpu.VMEM(((h + 2) * wp, c1), F32),
        pltpu.VMEM(((h + 2) * wpc, c2), F32),
        pltpu.VMEM(((h + 4) * wpc, c2), F32),
        pltpu.VMEM(((h + 2) * wpc, 3 * c2), BF16),
        pltpu.VMEM((2, (h + 6) * wpc, 128), F32),
        pltpu.VMEM(((h + 4) * wpc, 3 * c2), BF16),
        pltpu.VMEM(((h + 2) * wpc, c2), F32),
        pltpu.VMEM(((H + 6) * wp, c1), F32),
        pltpu.VMEM(((H + 4) * wp, 3 * c1), BF16),
        pltpu.VMEM(((H + 1) * wp, c1), F32),
        pltpu.VMEM((2, 3 * wp + 4 * wpc, 128), BF16),
        pltpu.VMEM((2, 3 * H + 4 * h, 128), BF16),
        pltpu.VMEM((8, 3 * wp + 4 * wpc, 128), BF16),
        pltpu.VMEM((2, 3 * H + 4 * h, 128), BF16),
        pltpu.VMEM((2, ngx, 2, 128), F32),
        pltpu.VMEM((2, ngx, 4, 128), F32),
        pltpu.VMEM((2, ngy, 2, 128), F32),
        pltpu.VMEM((2, ngy, 4, 128), F32),
        pltpu.VMEM((rows_c, 128), BF16), pltpu.VMEM((rows_c, 128), BF16), *landings(rows_c),
        pltpu.VMEM((rows_b, 128), BF16), pltpu.VMEM((rows_b, 128), BF16),
        *landings(rows_b, (2, ngy, ngx // 2)),
        pltpu.VMEM((rows_f, 128), BF16), pltpu.VMEM((rows_f, 128), BF16), *landings(rows_f),
        DMA((8,)), DMA((8,)),
        DMA((4, ngx)), DMA((4, ngx)), DMA((4, ngy)), DMA((4, ngy)),
        *[DMA((6, most))] * 6,
    ]
    def shapes(kind):
        return (
            jax.ShapeDtypeStruct((h, w, c2), BF16),
            jax.ShapeDtypeStruct((H, W, c1), BF16),
            jax.ShapeDtypeStruct((9 * c1, c1), kind),
            jax.ShapeDtypeStruct((1, c1), F32),
            jax.ShapeDtypeStruct((c1, c2), kind),
            jax.ShapeDtypeStruct((9 * c2, c2), kind),
            jax.ShapeDtypeStruct((1, c2), F32),
        )

    hbm = pl.BlockSpec(memory_space=pltpu.HBM)
    results = pl.pallas_call(
        functools.partial(kernel, sizes),
        out_shape=shapes(BF16),
        in_specs=[hbm] * 7,
        out_specs=[hbm] * 7,
        scratch_shapes=[pltpu.VMEM(shape.shape, shape.dtype) for shape in shapes(BF16)]
        + [DMA((7,))] + scratch,
        compiler_params=pltpu.CompilerParams(
            collective_id=0, has_side_effects=True, vmem_limit_bytes=63 * 2**20),
    )(
        field, cotangent, gain_fine.reshape(1, c1), weight_fine.reshape(3, 3 * c1, c1),
        projection, gain_coarse.reshape(1, c2), weight_coarse.reshape(3, 3 * c2, c2),
    )
    cout, fgrad, wf_grad, gf_grad, proj_grad, wc_grad, gc_grad = pl.pallas_call(
        deliver,
        out_shape=shapes(F32),
        in_specs=[hbm] * 7,
        out_specs=[hbm] * 7,
        scratch_shapes=[pltpu.VMEM(shape.shape, shape.dtype) for shape in shapes(BF16)] + [
            pltpu.VMEM((9 * c2, c2), F32), pltpu.VMEM((9 * c1, c1), F32),
            pltpu.VMEM((c1, c2), F32), DMA((7,)), DMA((7,)),
        ],
        compiler_params=pltpu.CompilerParams(vmem_limit_bytes=63 * 2**20),
    )(*results)
    return (
        cout, fgrad, wf_grad.reshape(3, 3, c1, c1), gf_grad.reshape(c1), proj_grad,
        wc_grad.reshape(3, 3, c2, c2), gc_grad.reshape(c2),
    )


def solution(mesh):
    return jax.shard_map(
        on_device,
        mesh=mesh,
        in_specs=(P("gy", "gx", None), P("gy", "gx", None), P(), P(), P(), P(), P()),
        out_specs=(P("gy", "gx", None), P("gy", "gx", None), P(), P(), P(), P(), P()),
        check_vma=False,
    )
```

```python
import functools

import jax
import jax.numpy as jnp
from jax import lax
from jax.experimental import pallas as pl
from jax.experimental.pallas import tpu as pltpu
from jax.sharding import PartitionSpec as P

GROUPS = 32
EPSILON = 1e-05
F32 = jnp.float32
BF16 = jnp.bfloat16
MESH = pl.DeviceIdType.MESH
DIRS = ((1, 0), (-1, 0), (0, 1), (0, -1), (1, 1), (1, -1), (-1, 1), (-1, -1))


def round_up(value, unit):
    return -(-value // unit) * unit


def log2(value):
    assert value & (value - 1) == 0
    return value.bit_length() - 1


def cell_of(shape, pitch):
    index = lax.broadcasted_iota(jnp.int32, shape, 0)
    return lax.shift_right_logical(index, log2(pitch)), index & (pitch - 1)


def within(value, low, high):
    return (value >= low) & (value < high)


def group_sums(sums, per_group):
    channels = sums.shape[1]
    bits = log2(per_group)
    one = lax.broadcasted_iota(jnp.int32, (channels, channels), 0)
    two = lax.broadcasted_iota(jnp.int32, (channels, channels), 1)
    same = lax.shift_right_logical(one, bits) == lax.shift_right_logical(two, bits)
    high = sums.astype(BF16)
    rest = sums - high.astype(F32)
    middle = rest.astype(BF16)
    low = (rest - middle.astype(F32)).astype(BF16)
    count = sums.shape[0]
    pad = jnp.zeros((16 - 3 * count, channels), F32)
    parts = jnp.concatenate(
        [high.astype(F32), middle.astype(F32), low.astype(F32), pad], axis=0).astype(BF16)
    total = jnp.dot(parts, same.astype(F32).astype(BF16), preferred_element_type=F32)
    return total[0:count] + total[count:2 * count] + total[2 * count:3 * count]


def sigmoid(act):
    return 0.5 + 0.5 * jnp.tanh(0.5 * act)


def fold(values):
    return jnp.sum(values.reshape(-1, 8, values.shape[1]), axis=0)


def unfold(partial):
    return jnp.sum(partial, axis=0, keepdims=True)


def matmul_nt(left, right):
    return lax.dot_general(left, right, (((1,), (1,)), ((), ())), preferred_element_type=F32)


def matmul_tn(left, right):
    return lax.dot_general(left, right, (((0,), (0,)), ((), ())), preferred_element_type=F32)


def split_rows(sums):
    return jnp.concatenate([sums[:, :128], sums[:, 128:]], axis=0)


class Reducer:
    def __init__(self, levels, rows, data, full, landings, sends, recvs):
        self.levels, self.rows = levels, rows
        self.data, self.full, self.landings = data, full, landings
        self.sends, self.recvs = sends, recvs

    def span(self, base, count):
        return pl.ds(pl.multiple_of(base, 16), count)

    def offset(self, depth):
        base, size = 0, self.rows
        for _, count, index, _ in self.levels[:depth]:
            size //= count
            base = base + index * size
        return base, size

    def copies(self, stage):
        depth = len(self.levels)
        gather = stage >= depth
        level = 2 * depth - 1 - stage if gather else stage
        _, count, index, device = self.levels[level]
        base, size = self.offset(level)
        part = size // count
        out = []
        for step in range(1, count):
            peer = lax.rem(index + step, count)
            if gather:
                own = self.full.at[self.span(base + index * part, part)]
                src, dst, theirs = own, own, self.full.at[self.span(base + peer * part, part)]
            else:
                src = self.data.at[self.span(base + peer * part, part)]
                dst = self.landings[level].at[index]
                theirs = self.landings[level].at[peer]
            out.append((
                pltpu.make_async_remote_copy(
                    src_ref=src, dst_ref=dst,
                    send_sem=self.sends.at[stage, step], recv_sem=self.recvs.at[stage, index],
                    device_id=device(peer), device_id_type=MESH,
                ),
                pltpu.make_async_remote_copy(
                    src_ref=theirs, dst_ref=theirs,
                    send_sem=self.sends.at[stage, step], recv_sem=self.recvs.at[stage, peer],
                    device_id=device(peer), device_id_type=MESH,
                ),
            ))
        return out

    def start(self, stage):
        for copy, _ in self.copies(stage):
            copy.start()

    def finish(self, stage):
        depth = len(self.levels)
        for copy, arrival in self.copies(stage):
            copy.wait_send()
            arrival.wait_recv()
        if stage < depth:
            _, count, index, _ = self.levels[stage]
            base, size = self.offset(stage)
            part = size // count
            mine = self.span(base + index * part, part)
            landing = self.landings[stage]
            landing[index] = self.data[mine]
            total = landing[0].astype(F32)
            for source in range(1, count):
                total = total + landing[source].astype(F32)
            target = self.full if stage == depth - 1 else self.data
            target[mine] = total.astype(BF16)


class Pair:
    def __init__(self, *members):
        self.members = members

    def start(self, stage):
        for member in self.members:
            member.start(stage)

    def finish(self, stage):
        for member in self.members:
            member.finish(stage)


def kernel(sizes, field_h, cot_h, gain_f_h, wf_h, proj_h, gain_c_h, wc_h,
           cout_h, fgrad_h, wf_grad_h, gf_grad_h, proj_grad_h, wc_grad_h, gc_grad_h,
           cout, fgrad, wf_grad, gf_grad, proj_grad, wc_grad, gc_grad, store_sem,
           field, cot, gain_f, wf, proj, gain_c, wc, load_sem,
           E, HF, X3f, PU, CI, HC, X3c, C, X3g, DC, D, X3d, T,
           row_out, col_out, row_in, col_in, slots_f, slots_c,
           data_c, full_c, lc1, lc2, lc3, data_b, full_b, lb1, lb2, lb3, data_f, full_f, lf1, lf2, lf3,
           rim_send, rim_recv, sum_send, sum_recv, c_send, c_recv, b_send, b_recv, f_send, f_recv):
    H, W, h, w, wp, wpc, ngy, ngx = sizes
    c1, c2 = proj.shape
    count_all = ngy * ngx
    gy, gx = lax.axis_index("gy"), lax.axis_index("gx")
    me = gy * ngx + gx
    fine_count = float(H * W * count_all * (c1 // GROUPS))
    coarse_count = float(h * w * count_all * (c2 // GROUPS))

    def wrapped(place, count):
        return jnp.where(place >= count, place - count, place)

    few = count_all <= 64
    if few:
        rows_of = [wrapped(gy + dy, ngy) for dy in range(ngy)]
        cols_of = [wrapped(gx + dx, ngx) for dx in range(ngx)]

    def peer_of(step):
        if few:
            place = (rows_of[step // ngx], cols_of[step % ngx])
            return place[0] * ngx + place[1], place
        peer = lax.rem(me + step, count_all)
        return peer, (lax.div(peer, ngx), lax.rem(peer, ngx))

    def each_peer(body):
        if few:
            for step in range(1, count_all):
                body(step)
        else:
            pl.loop(1, count_all)(body)

    loads = [
        pltpu.make_async_copy(src, dst, load_sem.at[number])
        for number, (src, dst) in enumerate(zip(
            (field_h, cot_h, gain_f_h, wf_h, proj_h, gain_c_h, wc_h),
            (field, cot, gain_f, wf, proj, gain_c, wc)))
    ]
    for number in (0, 1, 6, 2, 3, 4, 5):
        loads[number].start()
    stores = [
        pltpu.make_async_copy(src, dst, store_sem.at[number])
        for number, (src, dst) in enumerate(zip(
            (cout, fgrad, wf_grad, gf_grad, proj_grad, wc_grad, gc_grad),
            (cout_h, fgrad_h, wf_grad_h, gf_grad_h, proj_grad_h, wc_grad_h, gc_grad_h)))
    ]
    barrier = pltpu.get_barrier_semaphore()

    def greet(step):
        pl.semaphore_signal(barrier, inc=1, device_id=peer_of(step)[1], device_id_type=MESH)

    each_peer(greet)

    def slots_of(turn):
        return (slots_c if turn in (1, 2) else slots_f).at[turn // 2]

    def sum_copy(turn, step):
        peer, device = peer_of(step)
        slots = slots_of(turn)
        go = pltpu.make_async_remote_copy(
            src_ref=slots.at[me], dst_ref=slots.at[me],
            send_sem=sum_send.at[step], recv_sem=sum_recv.at[turn % 2, me],
            device_id=device, device_id_type=MESH)
        come = pltpu.make_async_remote_copy(
            src_ref=slots.at[peer], dst_ref=slots.at[peer],
            send_sem=sum_send.at[step], recv_sem=sum_recv.at[turn % 2, peer],
            device_id=device, device_id_type=MESH)
        return go, come

    def sums_start(turn, rows):
        slots_of(turn)[me] = rows

        each_peer(lambda step: sum_copy(turn, step)[0].start())

    def sums_finish(turn):
        def settle(step):
            go, come = sum_copy(turn, step)
            go.wait_send()
            come.wait_recv()

        each_peer(settle)
        return jnp.sum(slots_of(turn)[...], axis=0)

    loads[0].wait()
    values = field[...].astype(F32)
    sums_f = jnp.concatenate([
        jnp.sum(values, axis=(0, 1), keepdims=True).reshape(1, c1),
        jnp.sum(values * values, axis=(0, 1), keepdims=True).reshape(1, c1)], axis=0)
    E[...] = jnp.zeros(E.shape, F32)
    E[pl.ds(3 * wp + 3, H * wp), :] = jnp.concatenate(
        [values, jnp.zeros((H, wp - W, c1), F32)], axis=1).reshape(H * wp, c1)
    loads[1].wait()
    grads = jnp.concatenate([cot[...].astype(F32), jnp.zeros((h, wpc - w, c2), F32)], axis=1)
    grads = grads.reshape(h * wpc, c2)
    C[...] = jnp.zeros(C.shape, F32)
    for half in range(2):
        C[half, pl.ds(2 * wpc + 2, h * wpc), :] = grads[:, half * 128:(half + 1) * 128]

    fr, cr = 3 * wp, 2 * wpc
    for side, (first, first_c) in enumerate(((H, h), (3, 2))):
        row_out[side, 0:fr] = E[first * wp:first * wp + fr].astype(BF16)
        for half in range(2):
            row_out[side, fr + half * cr:fr + (half + 1) * cr] = (
                C[half, first_c * wpc:first_c * wpc + cr].astype(BF16))
    for side, (first, first_c) in enumerate(((W, w), (3, 2))):
        for col in range(3):
            col_out[side, col * H:(col + 1) * H] = (
                E[pl.ds(3 * wp + first + col, H, stride=wp), :].astype(BF16))
        for half in range(2):
            for col in range(2):
                at = 3 * H + (2 * half + col) * h
                col_out[side, at:at + h] = (
                    C[half, pl.ds(2 * wpc + first_c + col, h, stride=wpc), :].astype(BF16))

    pl.semaphore_wait(barrier, count_all - 1)
    sums_start(0, sums_f)

    def rim_copy(number):
        dy, dx = DIRS[number]
        if dy != 0:
            src = row_out.at[0 if dy > 0 else 1]
            dst = row_in.at[number]
        else:
            src = col_out.at[0 if dx > 0 else 1]
            dst = col_in.at[number - 2]
        return pltpu.make_async_remote_copy(
            src_ref=src, dst_ref=dst, send_sem=rim_send.at[number], recv_sem=rim_recv.at[number],
            device_id=(gy + dy, gx + dx), device_id_type=MESH)

    def reaches(dy, dx):
        return within(gy + dy, 0, ngy) & within(gx + dx, 0, ngx)

    for number, (dy, dx) in enumerate(DIRS):
        @pl.when(reaches(dy, dx))
        def _():
            rim_copy(number).start()

    _, col_f = cell_of((fr, 128), wp)
    _, col_c = cell_of((cr, 128), wpc)

    def place(piece, dx, width, rim, cols):
        if dx == 0:
            return piece
        gap = jnp.zeros((width, 128), F32)
        if dx > 0:
            return jnp.where(cols < rim, jnp.concatenate([piece[width:], gap], axis=0), 0.0)
        moved = jnp.concatenate([gap, piece[:piece.shape[0] - width]], axis=0)
        return jnp.where(within(cols, width + rim, width + 2 * rim), moved, 0.0)

    for number, (dy, dx) in enumerate(DIRS):
        @pl.when(reaches(-dy, -dx))
        def _():
            rim_copy(number).wait_recv()
            if dy != 0:
                at = 0 if dy > 0 else (H + 3) * wp
                piece = row_in[number, 0:fr].astype(F32)
                E[at:at + fr] = E[at:at + fr] + place(piece, dx, W, 3, col_f)
                at = 0 if dy > 0 else (h + 2) * wpc
                for half in range(2):
                    piece = row_in[number, fr + half * cr:fr + (half + 1) * cr].astype(F32)
                    C[half, at:at + cr] = C[half, at:at + cr] + place(piece, dx, w, 2, col_c)
            else:
                at = 0 if dx > 0 else W + 3
                for col in range(3):
                    E[pl.ds(3 * wp + at + col, H, stride=wp), :] = (
                        col_in[number - 2, col * H:(col + 1) * H].astype(F32))
                at = 0 if dx > 0 else w + 2
                for half in range(2):
                    for col in range(2):
                        row = 3 * H + (2 * half + col) * h
                        C[half, pl.ds(2 * wpc + at + col, h, stride=wpc), :] = (
                            col_in[number - 2, row:row + h].astype(F32))

    ext = (h + 2) * wpc
    for tap in range(3):
        for half in range(2):
            at = tap * c2 + half * 128
            for go in range(0, (h + 4) * wpc, 4 * wpc):
                X3g[go:go + 4 * wpc, at:at + 128] = (
                    C[half, pl.ds(tap + go, 4 * wpc), :].astype(BF16))
    loads[6].wait()
    cells = jnp.concatenate([X3g[a * wpc:a * wpc + ext, :] for a in range(3)], axis=1)
    taps = jnp.concatenate(
        [wc[2 - a, (2 - b) * c2:(3 - b) * c2, :] for a in range(3) for b in range(3)], axis=1)
    DC[...] = matmul_nt(cells, taps)

    for number in (2, 3, 4, 5):
        loads[number].wait()
    total = group_sums(sums_finish(0), c1 // GROUPS)
    avg_f = total[0:1] / fine_count
    inv_f = lax.rsqrt(total[1:2] / fine_count - avg_f * avg_f + EPSILON)
    gain = gain_f[...]
    scale_f = inv_f * gain
    shift_f = -avg_f * scale_f
    row, col = cell_of((4 * wp, c1), wp)
    col_inside = within(col + (gx * W - 3), 0, W * ngx)
    for go in range(0, (H + 8) * wp, 4 * wp):
        act = E[go:go + 4 * wp] * scale_f + shift_f
        inside = col_inside & within(row + (gy * H - 3 + go // wp), 0, H * ngy)
        HF[go:go + 4 * wp] = jnp.where(inside, act * sigmoid(act), 0.0)
    for tap in range(3):
        for go in range(0, (H + 6) * wp, 2 * wp):
            X3f[go:go + 2 * wp, tap * c1:(tap + 1) * c1] = (
                HF[pl.ds(tap + go, 2 * wp), :].astype(BF16))
    span = (H + 4) * wp
    cells = jnp.concatenate([X3f[a * wp:a * wp + span, :] for a in range(3)], axis=1)
    HF[0:span] = jnp.dot(cells, wf[...].reshape(9 * c1, c1), preferred_element_type=F32)
    for go in range(0, span, 4 * wp):
        block = HF[go:go + 4 * wp] + E[pl.ds(wp + 1 + go, 4 * wp), :]
        block = block.astype(BF16).astype(F32).reshape(2, 2, wp, c1)
        PU[go // 2:go // 2 + 2 * wp] = (block[:, 0] + block[:, 1]).reshape(2 * wp, c1)
    pooled = ((PU[pl.ds(0, ext, stride=2), :] + PU[pl.ds(1, ext, stride=2), :]) * 0.25)
    prow, pcol = cell_of((ext, c1), wpc)
    inner_p = within(prow, 1, h + 1) & within(pcol, 1, w + 1)
    pooled_in = jnp.where(inner_p, pooled, 0.0).astype(BF16)
    coarse_in = jnp.dot(pooled.astype(BF16), proj[...], preferred_element_type=F32)
    coarse_in = coarse_in.astype(BF16).astype(F32)
    CI[...] = coarse_in
    step_c = 2 * wpc
    prow, pcol = cell_of((step_c, c2), wpc)
    pcol_inner = within(pcol, 1, w + 1)
    pcol_inside = within(pcol + (gx * w - 1), 0, w * ngx)

    def inner_at(go):
        return pcol_inner & within(prow + go // wpc, 1, h + 1)

    def inside_at(go):
        return pcol_inside & within(prow + (gy * h - 1 + go // wpc), 0, h * ngy)

    one, two = jnp.zeros((8, c2), F32), jnp.zeros((8, c2), F32)
    for go in range(0, ext, step_c):
        kept = jnp.where(inner_at(go), CI[go:go + step_c], 0.0)
        one, two = one + fold(kept), two + fold(kept * kept)
    sums_start(1, split_rows(jnp.concatenate([unfold(one), unfold(two)], axis=0)))

    def joined(rows):
        return jnp.concatenate([rows[0:2], rows[2:4]], axis=1)

    total = group_sums(joined(sums_finish(1)), c2 // GROUPS)
    avg_c = total[0:1] / coarse_count
    inv_c = lax.rsqrt(total[1:2] / coarse_count - avg_c * avg_c + EPSILON)
    gain2 = gain_c[...]
    one, two = jnp.zeros((8, c2), F32), jnp.zeros((8, c2), F32)
    for go in range(0, ext, step_c):
        norm_c = (CI[go:go + step_c] - avg_c) * inv_c
        act = norm_c * gain2
        sigma = sigmoid(act)
        dact_c = DC[go:go + step_c] * (sigma * (1.0 + act * (1.0 - sigma)))
        DC[go:go + step_c] = dact_c
        kept = jnp.where(inner_at(go), dact_c, 0.0)
        one, two = one + fold(kept), two + fold(kept * norm_c)
        HC[go:go + step_c] = jnp.where(inside_at(go), act * sigma, 0.0)
    sums_start(2, split_rows(jnp.concatenate([unfold(one), unfold(two)], axis=0)))
    HC[ext:] = jnp.zeros((HC.shape[0] - ext, c2), F32)
    for tap in range(3):
        for go in range(0, ext, step_c):
            X3c[go:go + step_c, tap * c2:(tap + 1) * c2] = (
                HC[pl.ds(tap + go, step_c), :].astype(BF16))
    cells_c = h * wpc
    gb = grads.T.astype(BF16)
    taps_c = 3 * c2
    for a in range(3):
        part = jnp.dot(gb, X3c[a * wpc:a * wpc + cells_c, :], preferred_element_type=F32)
        part = part.T.astype(BF16)
        target, base = (data_c, a * 2 * taps_c) if a < 2 else (data_b, 0)
        for half in range(2):
            at = base + half * taps_c
            target[at:at + taps_c] = part[:, half * 128:(half + 1) * 128]
    for target, used in ((data_c, 4 * taps_c), (data_b, 2 * taps_c)):
        if target.shape[0] > used:
            target[used:] = jnp.zeros((target.shape[0] - used, 128), BF16)

    core, chip = lax.rem(gx, 2), lax.div(gx, 2)
    levels = (
        ("core", 2, core, lambda k: (gy, chip * 2 + k)),
        ("chip", ngx // 2, chip, lambda k: (gy, k * 2 + core)),
        ("gy", ngy, gy, lambda k: (k, gx)),
    )
    turned = (levels[0], levels[2], levels[1])
    big = Pair(
        Reducer(levels, data_c.shape[0], data_c, full_c, (lc1, lc2, lc3), c_send, c_recv),
        Reducer(turned, data_b.shape[0], data_b, full_b, (lb1, lb2, lb3), b_send, b_recv))
    small = Reducer(levels, data_f.shape[0], data_f, full_f, (lf1, lf2, lf3), f_send, f_recv)
    big.start(0)

    cells = jnp.concatenate([X3c[a * wpc:a * wpc + cells_c, :] for a in range(3)], axis=1)
    HC[0:cells_c] = jnp.dot(cells, wc[...].reshape(9 * c2, c2), preferred_element_type=F32)
    for go in range(0, cells_c, step_c):
        out = HC[go:go + step_c] + CI[pl.ds(wpc + 1 + go, step_c), :]
        cout[go // wpc:go // wpc + 2] = out.reshape(2, wpc, c2)[:, :w].astype(BF16)
    stores[0].start()

    big.finish(0)
    big.start(1)

    total = joined(sums_finish(2))
    gc_grad[...] = total[1:2]
    stores[6].start()
    total = group_sums(total[0:2] * gain2, c2 // GROUPS)
    first, second = total[0:1] / coarse_count, total[1:2] / coarse_count
    scale_c = inv_c * gain2
    for go in range(0, ext, step_c):
        norm_c = (CI[go:go + step_c] - avg_c) * inv_c
        dcoarse = DC[go:go + step_c] * scale_c - inv_c * (first + norm_c * second)
        dcoarse = dcoarse + jnp.concatenate(
            [C[half, pl.ds(wpc + 1 + go, step_c), :] for half in range(2)], axis=1)
        X3g[go:go + step_c, 0:c2] = jnp.where(inside_at(go), dcoarse, 0.0).astype(BF16)
    dcoarse = X3g[0:ext, 0:c2]
    pgrad = matmul_tn(pooled_in, dcoarse).astype(BF16)
    taps_f = 9 * c1
    for half in range(2):
        at = taps_f + half * c1
        data_f[at:at + c1] = pgrad[:, half * 128:(half + 1) * 128]
    if data_f.shape[0] > taps_f + 2 * c1:
        data_f[taps_f + 2 * c1:] = jnp.zeros((data_f.shape[0] - taps_f - 2 * c1, 128), BF16)
    dsmall = (matmul_nt(dcoarse, proj[...]) * 0.25).astype(BF16).astype(F32)
    PU[pl.ds(0, ext, stride=2), :] = dsmall
    PU[pl.ds(1, ext, stride=2), :] = dsmall
    for pair in range(h + 2):
        wide = PU[pair * wp:(pair + 1) * wp]
        D[2 * pair * wp:(2 * pair + 1) * wp] = wide
        D[(2 * pair + 1) * wp:(2 * pair + 2) * wp] = wide
    D[span:] = jnp.zeros((D.shape[0] - span, c1), F32)
    cells_f = H * wp
    _, col = cell_of((cells_f, c1), wp)
    gm = jnp.where(within(col, 2, W + 2), D[2 * wp:2 * wp + cells_f], 0.0).T.astype(BF16)
    for a in range(3):
        part = jnp.dot(gm, X3f[(2 + a) * wp:(2 + a) * wp + cells_f, :], preferred_element_type=F32)
        data_f[a * 3 * c1:(a + 1) * 3 * c1] = part.T.astype(BF16)
    small.start(0)
    big.finish(1)
    big.start(2)
    for tap in range(3):
        for go in range(0, span, 4 * wp):
            X3d[go:go + 4 * wp, tap * c1:(tap + 1) * c1] = (
                D[pl.ds(tap + go, 4 * wp), :].astype(BF16))
    cells = jnp.concatenate(
        [X3d[(1 + a) * wp:(1 + a) * wp + cells_f, :] for a in range(3)], axis=1)
    taps = jnp.concatenate(
        [wf[2 - a, (2 - b) * c1:(3 - b) * c1, :] for a in range(3) for b in range(3)], axis=1)
    T[0:cells_f] = matmul_nt(cells, taps)
    _, col = cell_of((4 * wp, c1), wp)
    own_col = within(col, 1, W + 1)
    one, two = jnp.zeros((8, c1), F32), jnp.zeros((8, c1), F32)
    for go in range(0, cells_f, 4 * wp):
        norm_f = (E[pl.ds(3 * wp + 2 + go, 4 * wp), :] - avg_f) * inv_f
        act = norm_f * gain
        sigma = sigmoid(act)
        dact = T[go:go + 4 * wp] * (sigma * (1.0 + act * (1.0 - sigma)))
        T[go:go + 4 * wp] = dact
        kept = jnp.where(own_col, dact, 0.0)
        one, two = one + fold(kept), two + fold(kept * norm_f)
    sums_start(3, jnp.concatenate([unfold(one), unfold(two)], axis=0))

    small.finish(0)
    small.start(1)
    big.finish(2)
    big.start(3)

    total = sums_finish(3)
    big.finish(3)
    big.start(4)
    small.finish(1)
    small.start(2)
    gf_grad[...] = total[1:2]
    stores[3].start()
    total = group_sums(total * gain, c1 // GROUPS)
    first, second = total[0:1] / fine_count, total[1:2] / fine_count
    T[cells_f:] = jnp.zeros((T.shape[0] - cells_f, c1), F32)
    for go in range(0, cells_f, 4 * wp):
        norm_f = (E[pl.ds(3 * wp + 2 + go, 4 * wp), :] - avg_f) * inv_f
        result = T[go:go + 4 * wp] * scale_f - inv_f * (first + norm_f * second)
        T[go:go + 4 * wp] = result + D[pl.ds(2 * wp + 1 + go, 4 * wp), :]
    for go in range(0, cells_f, 4 * wp):
        result = T[pl.ds(1 + go, 4 * wp), :].reshape(4, wp, c1)
        fgrad[go // wp:go // wp + 4] = result[:, :W].astype(BF16)
    stores[1].start()

    small.finish(2)
    small.start(3)
    small.finish(3)
    small.start(4)
    big.finish(4)
    big.start(5)
    small.finish(4)
    small.start(5)
    big.finish(5)
    for a in range(3):
        source, base = (full_c, a * 2 * taps_c) if a < 2 else (full_b, 0)
        for half in range(2):
            at = base + half * taps_c
            wc_grad[a * taps_c:(a + 1) * taps_c, half * 128:(half + 1) * 128] = (
                source[at:at + taps_c])
    stores[5].start()
    small.finish(5)
    wf_grad[...] = full_f[0:taps_f]
    stores[2].start()
    for half in range(2):
        at = taps_f + half * c1
        proj_grad[:, half * 128:(half + 1) * 128] = full_f[at:at + c1]
    stores[4].start()
    for copy in stores:
        copy.wait()

    for number, (dy, dx) in enumerate(DIRS):
        @pl.when(reaches(dy, dx))
        def _():
            rim_copy(number).wait_send()


def deliver(cout, fgrad, wf_grad, gf_grad, proj_grad, wc_grad, gc_grad, *rest):
    outs, held, wide, load_sem, store_sem = rest[:7], rest[7:14], rest[14:17], rest[17], rest[18]
    sources = (cout, fgrad, wf_grad, gf_grad, proj_grad, wc_grad, gc_grad)
    ready = list(held)
    ready[5], ready[2], ready[4] = wide
    order = (5, 2, 4, 1, 0, 3, 6)
    loads = [pltpu.make_async_copy(sources[k], held[k], load_sem.at[k]) for k in range(7)]
    stores = [pltpu.make_async_copy(ready[k], outs[k], store_sem.at[k]) for k in range(7)]
    for k in order:
        loads[k].start()
    for k in order:
        loads[k].wait()
        if ready[k] is not held[k]:
            ready[k][...] = held[k][...].astype(F32)
        stores[k].start()
    for k in order:
        stores[k].wait()


def on_device(field, cotangent, gain_fine, weight_fine, projection, gain_coarse, weight_coarse):
    H, W, c1 = field.shape
    h, w, c2 = cotangent.shape
    ngy, ngx = lax.axis_size("gy"), lax.axis_size("gx")
    everyone = ngy * ngx
    wpc = round_up(w + 4, 16)
    wp = 2 * wpc
    sizes = (H, W, h, w, wp, wpc, ngy, ngx)
    rows_c = everyone * round_up(-(-12 * c2 // everyone), 16)
    rows_b = everyone * round_up(-(-6 * c2 // everyone), 16)
    rows_f = everyone * round_up(-(-11 * c1 // everyone), 16)
    counts = (2, ngx // 2, ngy)
    most = max(counts)

    def landings(rows, order=counts):
        out = []
        for count in order:
            rows //= count
            out.append(pltpu.VMEM((count, rows, 128), BF16))
        return out

    DMA = pltpu.SemaphoreType.DMA
    scratch = [
        pltpu.VMEM((H, W, c1), BF16),
        pltpu.VMEM((h, w, c2), BF16),
        pltpu.VMEM((1, c1), F32),
        pltpu.VMEM((3, 3 * c1, c1), BF16),
        pltpu.VMEM((c1, c2), BF16),
        pltpu.VMEM((1, c2), F32),
        pltpu.VMEM((3, 3 * c2, c2), BF16),
        DMA((7,)),
        pltpu.VMEM(((H + 8) * wp, c1), F32),
        pltpu.VMEM(((H + 8) * wp, c1), F32),
        pltpu.VMEM(((H + 6) * wp, 3 * c1), BF16),
        pltpu.VMEM(((h + 2) * wp, c1), F32),
        pltpu.VMEM(((h + 2) * wpc, c2), F32),
        pltpu.VMEM(((h + 4) * wpc, c2), F32),
        pltpu.VMEM(((h + 2) * wpc, 3 * c2), BF16),
        pltpu.VMEM((2, (h + 6) * wpc, 128), F32),
        pltpu.VMEM(((h + 4) * wpc, 3 * c2), BF16),
        pltpu.VMEM(((h + 2) * wpc, c2), F32),
        pltpu.VMEM(((H + 6) * wp, c1), F32),
        pltpu.VMEM(((H + 4) * wp, 3 * c1), BF16),
        pltpu.VMEM(((H + 1) * wp, c1), F32),
        pltpu.VMEM((2, 3 * wp + 4 * wpc, 128), BF16),
        pltpu.VMEM((2, 3 * H + 4 * h, 128), BF16),
        pltpu.VMEM((8, 3 * wp + 4 * wpc, 128), BF16),
        pltpu.VMEM((2, 3 * H + 4 * h, 128), BF16),
        pltpu.VMEM((2, everyone, 2, 128), F32),
        pltpu.VMEM((2, everyone, 4, 128), F32),
        pltpu.VMEM((rows_c, 128), BF16), pltpu.VMEM((rows_c, 128), BF16), *landings(rows_c),
        pltpu.VMEM((rows_b, 128), BF16), pltpu.VMEM((rows_b, 128), BF16),
        *landings(rows_b, (2, ngy, ngx // 2)),
        pltpu.VMEM((rows_f, 128), BF16), pltpu.VMEM((rows_f, 128), BF16), *landings(rows_f),
        DMA((8,)), DMA((8,)),
        DMA((everyone,)), DMA((2, everyone)),
        *[DMA((6, most))] * 6,
    ]
    def shapes(kind):
        return (
            jax.ShapeDtypeStruct((h, w, c2), BF16),
            jax.ShapeDtypeStruct((H, W, c1), BF16),
            jax.ShapeDtypeStruct((9 * c1, c1), kind),
            jax.ShapeDtypeStruct((1, c1), F32),
            jax.ShapeDtypeStruct((c1, c2), kind),
            jax.ShapeDtypeStruct((9 * c2, c2), kind),
            jax.ShapeDtypeStruct((1, c2), F32),
        )

    hbm = pl.BlockSpec(memory_space=pltpu.HBM)
    results = pl.pallas_call(
        functools.partial(kernel, sizes),
        out_shape=shapes(BF16),
        in_specs=[hbm] * 7,
        out_specs=[hbm] * 7,
        scratch_shapes=[pltpu.VMEM(shape.shape, shape.dtype) for shape in shapes(BF16)]
        + [DMA((7,))] + scratch,
        compiler_params=pltpu.CompilerParams(
            collective_id=0, has_side_effects=True, vmem_limit_bytes=63 * 2**20),
    )(
        field, cotangent, gain_fine.reshape(1, c1), weight_fine.reshape(3, 3 * c1, c1),
        projection, gain_coarse.reshape(1, c2), weight_coarse.reshape(3, 3 * c2, c2),
    )
    cout, fgrad, wf_grad, gf_grad, proj_grad, wc_grad, gc_grad = pl.pallas_call(
        deliver,
        out_shape=shapes(F32),
        in_specs=[hbm] * 7,
        out_specs=[hbm] * 7,
        scratch_shapes=[pltpu.VMEM(shape.shape, shape.dtype) for shape in shapes(BF16)] + [
            pltpu.VMEM((9 * c2, c2), F32), pltpu.VMEM((9 * c1, c1), F32),
            pltpu.VMEM((c1, c2), F32), DMA((7,)), DMA((7,)),
        ],
        compiler_params=pltpu.CompilerParams(vmem_limit_bytes=63 * 2**20),
    )(*results)
    return (
        cout, fgrad, wf_grad.reshape(3, 3, c1, c1), gf_grad.reshape(c1), proj_grad,
        wc_grad.reshape(3, 3, c2, c2), gc_grad.reshape(c2),
    )


def solution(mesh):
    return jax.shard_map(
        on_device,
        mesh=mesh,
        in_specs=(P("gy", "gx", None), P("gy", "gx", None), P(), P(), P(), P(), P()),
        out_specs=(P("gy", "gx", None), P("gy", "gx", None), P(), P(), P(), P(), P()),
        check_vma=False,
    )
```
